32 devices in a mesh: tm: 4 (over x, core), space: 8 (over z, y).
Axes of the slice: x: 2, y: 2, z: 4, core: 2. Of those that a mesh axis runs over, the one named last changes fastest.
Arguments:
- start_states: float32 [4, 16, 64, 512], P('tm', 'space'), may hold values from -12 to 12
- diff_x: float32 [16, 64, 512], P('space'), may hold values from 0.3 to 3
- diff_y: float32 [16, 64, 512], P('space'), may hold values from 0.3 to 3
- diff_z: float32 [16, 64, 512], P('space'), may hold values from 0.3 to 3
- stress: float32 [16, 64, 512], P('space'), may hold values from -4 to 4
- trap_class: int32 [16, 64, 512], P('space'), may hold values from 0 to 3
- cotangent: float32 [4, 16, 64, 512], P('tm', 'space'), may hold values from -6 to 6
Outputs:
- new_ends: float32 [4, 16, 64, 512], P('tm', 'space')
- grad_x: float32 [16, 64, 512], P('space', 'tm')
- grad_y: float32 [16, 64, 512], P('space', 'tm')
- grad_z: float32 [16, 64, 512], P('space', 'tm')
- jump_norm: float32 [], replicated
The draws below stay inside these ranges and needn't reach their ends.
All inputs are finite; a program needn't handle non-finite values.
Results may differ from the reference program's by a relative error of at most 0.0003.
Values sent between devices are 32-bit elements; how exact they have to be, the bound alone decides.
No kernel may reach another device: no remote copies, remote signals or barrier semaphores. Data moves between devices by JAX's collectives and lax.ppermute only.
A program may use at most 192 MiB of HBM per device.

```python
import math
import jax
import jax.numpy as jnp
from jax import lax

NY = 64
NZ = 512
FINE_STEPS = 2
SWEEPS = 8
COARSE_SWEEPS = 2
NX = 16
SPANS = 4


def draw_start_states(key, part):
    span_ramp = jnp.sqrt(1.0 + 2.0 * jnp.arange(SPANS, dtype=jnp.float32) / max(SPANS - 1, 1))
    slab_ramp = jnp.sqrt(1.0 + 2.0 * jnp.arange(NX, dtype=jnp.float32) / max(NX - 1, 1))
    base_field = jax.random.truncated_normal(key, -4.0, 4.0, (SPANS, NX, NY, NZ), jnp.float32)
    return (base_field * span_ramp[:, None, None, None] * slab_ramp[None, :, None, None]).astype(jnp.float32)


def place_ends(drawn, stream_key, least, largest):
    extent = drawn.shape
    index_at = [jax.random.randint(jax.random.fold_in(stream_key, axis), (), 0, extent[axis]) for axis in range(len(extent))]
    drawn = drawn.at[tuple(index_at)].set(least)
    longest = extent.index(max(extent))
    index_at[longest] = (index_at[longest] + 1) % extent[longest]
    return drawn.at[tuple(index_at)].set(largest)


def spiked(entries, own_key, source, target, parts, factor):
    owner, partner = [(jnp.arange(entries.shape[axis_at]) // (entries.shape[axis_at] // parts)).reshape([-1 if axis == axis_at else 1 for axis in range(entries.ndim)]) for axis_at in (source, target)]
    chosen = jax.random.permutation(own_key, parts)[partner]
    strong = (owner == chosen) | (owner == (partner + parts // 2) % parts)
    return jnp.where(strong, factor * entries, entries)


def block_scale(stream_key, shape, cuts, low, high):
    def one(dim, blocks):
        steps = jax.random.uniform(jax.random.fold_in(jax.random.fold_in(stream_key, 6), dim), (blocks,), jnp.float32, low / len(cuts), high / len(cuts))
        return jnp.repeat(jnp.exp(steps), shape[dim] // blocks).reshape((-1,) + (1,) * (len(shape) - dim - 1))

    factor_of = one(*cuts[0])
    for cut in cuts[1:]:
        factor_of = factor_of * one(*cut)
    return factor_of


def centred(key, dims, scale, reach, shards=(), held_as=jnp.bfloat16):
    level = block_scale(key, dims, shards, -0.22, 0.18) if shards else 1.0
    drawn = jax.random.normal(key, dims, jnp.float32) * scale * level
    return jnp.minimum(jnp.maximum(drawn, -reach), reach).astype(held_as)


def noise_with(stream_key, shape, width, limit, cuts, heavy, held_as=jnp.bfloat16):
    values = width * jax.random.normal(stream_key, shape, jnp.float32)
    if cuts:
        values = values * block_scale(stream_key, shape, cuts, -0.22, 0.18)
    return jnp.clip(spiked(values, jax.random.fold_in(stream_key, 3), *heavy), -limit, limit).astype(held_as)


def setup_inputs(seed: int = 0) -> dict:
    arg_keys = jax.random.split(jax.random.key(seed), 8)
    start_states = draw_start_states(jax.random.fold_in(arg_keys[7], 71), 0)
    diff_x = jnp.clip(jnp.exp(math.log(3.0) - 2.3025851 * jax.random.uniform(arg_keys[1], (NX, NY, NZ), jnp.float32) ** block_scale(arg_keys[1], (NX, NY, NZ), ((0, 8),), -0.2, 0.2)), 0.3, 3.0)
    diff_y = jnp.clip(jnp.exp(math.log(3.0) - 2.3025851 * jax.random.uniform(arg_keys[2], (NX, NY, NZ), jnp.float32) ** block_scale(arg_keys[2], (NX, NY, NZ), ((0, 8),), -0.2, 0.2)), 0.3, 3.0)
    diff_z = jnp.clip(jnp.exp(math.log(3.0) - 2.3025851 * jax.random.uniform(arg_keys[3], (NX, NY, NZ), jnp.float32) ** block_scale(arg_keys[3], (NX, NY, NZ), ((0, 8),), -0.2, 0.2)), 0.3, 3.0)
    stress = centred(arg_keys[4], (NX, NY, NZ), 1.0, 4.0, ((0, 8),), jnp.float32)
    trap_class = place_ends(jax.random.randint(arg_keys[5], (NX, NY, NZ), 0, 4), jax.random.fold_in(arg_keys[5], 1), 0, 3).astype(jnp.int32)
    cotangent = noise_with(arg_keys[6], (SPANS, NX, NY, NZ), 1.0, 6.0, ((0, 4), (1, 8)), (0, 2, 4, 2.0), jnp.float32)
    return {"start_states": start_states, "diff_x": diff_x, "diff_y": diff_y, "diff_z": diff_z, "stress": stress, "trap_class": trap_class, "cotangent": cotangent}


stress_coupling = 0.5
time_step = 1.0
trap_levels = (0.0, 1.0, 3.0, 7.0)

def below_along(values_in, which_axis):
    length = values_in.shape[which_axis]
    zero_plane = jnp.zeros_like(lax.slice_in_dim(values_in, 0, 1, axis=which_axis))
    return jnp.concatenate([zero_plane, lax.slice_in_dim(values_in, 0, length - 1, axis=which_axis)], axis=which_axis)

def above_along(values_in, which_axis):
    length = values_in.shape[which_axis]
    zero_plane = jnp.zeros_like(lax.slice_in_dim(values_in, 0, 1, axis=which_axis))
    return jnp.concatenate([lax.slice_in_dim(values_in, 1, length, axis=which_axis), zero_plane], axis=which_axis)

def restrict(values_in):
    shaped = values_in.reshape(values_in.shape[0], values_in.shape[1] // 2, 2, values_in.shape[2] // 2, 2)
    return shaped.mean(axis=(2, 4))

def prolong(values_in):
    return jnp.repeat(jnp.repeat(values_in, 2, axis=1), 2, axis=2)

def trap_capacity(stress, trap_class):
    trap_level = jnp.zeros(stress.shape, stress.dtype)
    for position in range(len(trap_levels)):
        trap_level = trap_level + jnp.where(trap_class == position, trap_levels[position], 0.0).astype(stress.dtype)
    return (1.0 + trap_level) * jnp.exp(stress_coupling * stress)

def assemble(face_x, below_x, face_y, face_z, capacity, step_size):
    below_y = below_along(face_y, 1)
    below_z = below_along(face_z, 2)
    diagonal = capacity + step_size * (face_x + below_x + face_y + below_y + face_z + below_z)
    return (face_x, below_x, face_y, below_y, face_z, below_z, diagonal, capacity)

def coarse_coefficients(coeffs):
    return assemble(restrict(coeffs[0]), restrict(coeffs[1]), restrict(coeffs[2]) / 4.0, restrict(coeffs[4]) / 4.0, restrict(coeffs[7]), FINE_STEPS * time_step)

def neighbour_sum(padded, coeffs):
    centre = padded[1:-1]
    result = coeffs[0] * padded[2:] + coeffs[1] * padded[:-2]
    result = result + coeffs[2] * above_along(centre, 1) + coeffs[3] * below_along(centre, 1)
    result = result + coeffs[4] * above_along(centre, 2) + coeffs[5] * below_along(centre, 2)
    return result

def pad_first(values_in):
    return jnp.pad(values_in, ((1, 1), (0, 0), (0, 0)))

def propagate(start, coeffs):
    current = start
    for step_number in range(FINE_STEPS):
        source = coeffs[7] * current
        for sweep_number in range(SWEEPS):
            current = (source + time_step * neighbour_sum(pad_first(current), coeffs)) / coeffs[6]
    return current

def coarse_apply(start, coarse):
    source = coarse[7] * start
    current = start
    for sweep_number in range(COARSE_SWEEPS):
        current = (source + FINE_STEPS * time_step * neighbour_sum(pad_first(current), coarse)) / coarse[6]
    return current

def reference(start_states, diff_x, diff_y, diff_z, stress, trap_class, cotangent):
    capacity = trap_capacity(stress, trap_class)
    fine_ends = []
    grad_x = jnp.zeros(diff_x.shape, diff_x.dtype)
    grad_y = jnp.zeros(diff_x.shape, diff_x.dtype)
    grad_z = jnp.zeros(diff_x.shape, diff_x.dtype)
    for span in range(SPANS):
        span_start = start_states[span]

        def fine_map(face_x, face_y, face_z):
            coeffs = assemble(face_x, below_along(face_x, 0), face_y, face_z, capacity, time_step)
            return propagate(span_start, coeffs)
        span_end, pullback = jax.vjp(fine_map, diff_x, diff_y, diff_z)
        pieces = pullback(cotangent[span])
        grad_x = grad_x + pieces[0]
        grad_y = grad_y + pieces[1]
        grad_z = grad_z + pieces[2]
        fine_ends.append(span_end)
    coeffs = assemble(diff_x, below_along(diff_x, 0), diff_y, diff_z, capacity, time_step)
    coarse = coarse_coefficients(coeffs)
    coarse_state = jnp.zeros(restrict(start_states[0]).shape, diff_x.dtype)
    new_ends = []
    jump_total = jnp.zeros((), diff_x.dtype)
    for span in range(SPANS):
        correction = coarse_apply(coarse_state, coarse)
        new_ends.append(fine_ends[span] + prolong(correction))
        if span < SPANS - 1:
            jumps = restrict(fine_ends[span]) - restrict(start_states[span + 1])
            jump_total = jump_total + jnp.sum(jumps * jumps)
            coarse_state = jumps + correction
    jump_norm = jnp.sqrt(jump_total / ((SPANS - 1) * NX * (NY // 2) * (NZ // 2)))
    return (jnp.stack(new_ends), grad_x, grad_y, grad_z, jump_norm)
```

```python
import functools

import jax
import jax.numpy as jnp
from jax import lax
from jax.experimental import pallas as pl
from jax.experimental.pallas import tpu as pltpu
from jax.sharding import PartitionSpec as P

FINE_STEPS = 2
SWEEPS = 8
COARSE_SWEEPS = 2
TOTAL = FINE_STEPS * SWEEPS
LANES = 128
SUB = 8

STRESS_COUPLING = 0.5
TIME_STEP = 1.0
COARSE_STEP = FINE_STEPS * TIME_STEP
TRAP_LEVELS = (0.0, 1.0, 3.0, 7.0)

VMEM_BYTES = 56 * 1024 * 1024


class Sizes:
    def __init__(self, spans, space, planes, ny, nz):
        self.spans = spans
        self.space = space
        self.planes = planes
        self.nx = planes * space
        self.ny = ny
        self.nz = nz
        self.own = nz // space
        self.halo = (LANES - self.own) // 2
        self.quarter = ny // spans
        self.factor = LANES // self.own
        self.grad_parts = 3 * self.quarter // SUB
        self.grad_tiles = -(-self.grad_parts // self.factor)
        self.end_parts = ny // SUB
        self.end_tiles = self.end_parts // self.factor
        self.grad_rows = planes * self.grad_tiles * SUB
        self.end_rows = planes * self.end_tiles * SUB
        self.out_rows = self.grad_rows + self.end_rows + SUB
        assert TOTAL + 2 * COARSE_SWEEPS * (spans - 1) <= self.halo


def lane_of(shape):
    return lax.broadcasted_iota(jnp.int32, shape, len(shape) - 1)


def row_of(shape):
    return lax.broadcasted_iota(jnp.int32, shape, len(shape) - 2)


def z_up(v, by=1):
    return pltpu.roll(v, LANES - by, 1)


def z_down(v, by=1):
    return pltpu.roll(v, by, 1)


def roll_lanes(v, by):
    by = by % LANES
    return v if by == 0 else pltpu.roll(v, by, 1)


def windows_kernel(sz, start_ref, fx_ref, fy_ref, fz_ref, stress_ref, trap_ref, cot_ref, coef_out, start_out, cot_out):
    turn = lax.axis_index("tm")
    rows = pl.ds(pl.multiple_of(turn * sz.quarter, SUB), sz.quarter)
    tiles = sz.nz // LANES

    def cut(block_of, height, out_ref, row):
        parts = [block_of(n) for n in range(tiles)]
        lane = lane_of((height, LANES))
        for j in range(sz.space):
            first = sz.own * j - sz.halo
            tile, shift = first // LANES, first % LANES
            low = parts[tile] if 0 <= tile < tiles else None
            high = parts[tile + 1] if shift and tile + 1 < tiles else None
            zero = jnp.zeros((height, LANES), jnp.float32)
            low = zero if low is None else roll_lanes(low, -shift)
            if shift:
                high = zero if high is None else roll_lanes(high, -shift)
                low = jnp.where(lane < LANES - shift, low, high)
            out_ref[j, row : row + height, :] = low

    for p in range(sz.planes):
        span = lambda n: slice(n * LANES, (n + 1) * LANES)

        def capacity(n):
            trap = trap_ref[p, rows, span(n)]
            level = jnp.zeros(trap.shape, jnp.float32)
            for position, value in enumerate(TRAP_LEVELS):
                level = level + jnp.where(trap == position, value, 0.0)
            return (1.0 + level) * jnp.exp(STRESS_COUPLING * stress_ref[p, rows, span(n)])

        for f, ref in enumerate((fx_ref, fy_ref, fz_ref)):
            cut(lambda n: ref[p, rows, span(n)], sz.quarter, coef_out, (f * sz.planes + p) * sz.quarter)
        cut(capacity, sz.quarter, coef_out, (3 * sz.planes + p) * sz.quarter)
        for ref, out in ((start_ref, start_out), (cot_ref, cot_out)):
            for r in range(0, sz.ny, 16):
                cut(lambda n: ref[0, p, r : r + 16, span(n)], 16, out, p * sz.ny + r)


def valid_columns(sz):
    lane = lane_of((sz.ny, LANES))
    column = lax.axis_index("space") * sz.own - sz.halo + lane
    return (column >= 0) & (column < sz.nz)


def lay_out_faces(sz, pieces, faces):
    turn = lax.axis_index("tm")
    for key, piece in enumerate(pieces):
        rows = pl.ds(pl.multiple_of((turn ^ key) * sz.quarter, SUB), sz.quarter)
        for f in range(4):
            for p in range(sz.planes):
                first = (f * sz.planes + p) * sz.quarter
                for s in range(sz.space):
                    faces[f, s * sz.planes + p, rows, :] = piece[s, first : first + sz.quarter, :]


def row_down(v, by=1):
    return jnp.where(row_of(v.shape) < by, 0.0, pltpu.roll(v, by, 0))


def row_up(v, by=1):
    size = v.shape[0]
    return jnp.where(row_of(v.shape) >= size - by, 0.0, pltpu.roll(v, size - by, 0))


def averaged(v):
    lane, row = lane_of(v.shape), row_of(v.shape)
    v = v + jnp.where(lane % 2 == 0, z_up(v), z_down(v))
    size = v.shape[0]
    v = v + jnp.where(row % 2 == 0, pltpu.roll(v, size - 1, 0), pltpu.roll(v, 1, 0))
    return 0.25 * v


PAD = 8


def clear_rim(ref, at, nx, ny):
    zero = jnp.zeros((ny + 2 * PAD, LANES), jnp.float32)
    ref[at + (0,)] = zero
    ref[at + (nx + 1,)] = zero
    edge = jnp.zeros((PAD, LANES), jnp.float32)
    for i in range(1, nx + 1):
        ref[at + (i, slice(0, PAD))] = edge
        ref[at + (i, slice(PAD + ny, 2 * PAD + ny))] = edge


def fine_kernel(sz, *refs):
    pieces = refs[: sz.spans]
    start_ref, cot_ref, end_out, rough_out, grads_out = refs[sz.spans : sz.spans + 5]
    faces, coef, u, w, source, total, sx, sy, sz_acc, product = refs[sz.spans + 5 :]
    nx, ny = sz.nx, sz.ny
    body = slice(PAD, PAD + ny)
    XP, XM, YP, YM, ZP, ZM, CAP, INV = range(8)

    lay_out_faces(sz, pieces, faces)

    def clear_u(k, c):
        clear_rim(u, (k,), nx, ny)
        return c

    lax.fori_loop(0, TOTAL + 1, clear_u, 0)
    clear_rim(w, (0,), nx, ny)
    clear_rim(w, (1,), nx, ny)
    clear_rim(product, (), nx, ny)

    valid = valid_columns(sz)

    def normalise(i, c):
        fx, fy, fz, cap = (faces[f, i] for f in range(4))
        bx = jnp.where(i == 0, 0.0, faces[0, jnp.maximum(i - 1, 0)])
        by, bz = row_down(fy), z_down(fz)
        diagonal = cap + TIME_STEP * (fx + bx + fy + by + fz + bz)
        inv = jnp.where(valid, 1.0 / diagonal, 0.0)
        scaled = TIME_STEP * inv
        for n, face in ((XP, fx), (XM, bx), (YP, fy), (YM, by), (ZP, fz), (ZM, bz)):
            coef[n, i] = face * scaled
        coef[CAP, i] = cap * inv
        coef[INV, i] = inv
        return c

    lax.fori_loop(0, nx, normalise, 0)

    for s in range(sz.space):
        for p in range(sz.planes):
            i = s * sz.planes + p
            rows = slice(p * ny, (p + 1) * ny)
            u[0, i + 1, body, :] = start_ref[s, rows, :]
            w[0, i + 1, body, :] = coef[INV, i] * cot_ref[s, rows, :]

    def moved(i, ref, at):
        v = ref[at, i + 1, body, :]
        return (
            v,
            ref[at, i + 2, body, :],
            ref[at, i, body, :],
            ref[at, i + 1, PAD + 1 : PAD + 1 + ny, :],
            ref[at, i + 1, PAD - 1 : PAD - 1 + ny, :],
            z_up(v),
            z_down(v),
        )

    def gathered(i, near):
        result = coef[0, i] * near[0]
        for n in range(1, 6):
            result = result + coef[n, i] * near[n]
        return result

    for step in range(FINE_STEPS):
        base = step * SWEEPS

        def set_source(i, c):
            source[i] = coef[CAP, i] * u[base, i + 1, body, :]
            return c

        lax.fori_loop(0, nx, set_source, 0)

        def sweep(k, c):
            def plane(i, c):
                near = moved(i, u, k)
                u[k + 1, i + 1, body, :] = source[i] + gathered(i, near[1:])
                return c

            return lax.fori_loop(0, nx, plane, c)

        lax.fori_loop(base, base + SWEEPS, sweep, 0)

    lane, row = lane_of((SUB, LANES)), row_of((SUB, LANES))

    def finish(i, c):
        end = u[TOTAL, i + 1, body, :]
        end_out[i] = end
        rough_out[i] = packed(averaged(end))
        return c

    lax.fori_loop(0, nx, finish, 0)

    def zero_plane(i, c):
        zero = jnp.zeros((ny, LANES), jnp.float32)
        sx[i] = zero
        sy[i] = zero
        sz_acc[i] = zero
        product[i + 1, body, :] = zero
        return c

    lax.fori_loop(0, nx, zero_plane, 0)

    for step in reversed(range(FINE_STEPS)):
        base = step * SWEEPS

        def zero_total(i, c):
            total[i] = jnp.zeros((ny, LANES), jnp.float32)
            return c

        lax.fori_loop(0, nx, zero_total, 0)

        def back(n, c):
            k = base + SWEEPS - 1 - n
            now, later = n % 2, (n + 1) % 2

            def plane(i, c):
                near = moved(i, w, now)
                v, xp, yp, zp = near[0], near[1], near[3], near[5]
                field = u[k, i + 1, body, :]
                sx[i] = sx[i] + (v * u[k, i + 2, body, :] + xp * field)
                sy[i] = sy[i] + (v * u[k, i + 1, PAD + 1 : PAD + 1 + ny, :] + yp * field)
                sz_acc[i] = sz_acc[i] + (v * z_up(field) + zp * field)
                product[i + 1, body, :] = product[i + 1, body, :] + v * u[k + 1, i + 1, body, :]
                total[i] = total[i] + v
                w[later, i + 1, body, :] = gathered(i, near[1:])
                return c

            return lax.fori_loop(0, nx, plane, c)

        lax.fori_loop(0, SWEEPS, back, 0)

        if step:

            def restart(i, c):
                w[0, i + 1, body, :] = w[0, i + 1, body, :] + coef[CAP, i] * total[i]
                return c

            lax.fori_loop(0, nx, restart, 0)

    turn = lax.axis_index("tm")

    def write_grads(i, c):
        own = product[i + 1, body, :]
        dest, p = i // sz.planes, i % sz.planes
        sx[i] = TIME_STEP * (sx[i] - own - product[i + 2, body, :])
        sy[i] = TIME_STEP * (sy[i] - own - product[i + 1, PAD + 1 : PAD + 1 + ny, :])
        sz_acc[i] = TIME_STEP * (sz_acc[i] - own - z_up(own))
        for key in range(sz.spans):
            first = (turn ^ key) * sz.quarter
            for g in range(sz.grad_tiles):
                tile = None
                for q in range(sz.factor):
                    n = g * sz.factor + q
                    if n >= sz.grad_parts:
                        continue
                    f, r = divmod(n, sz.quarter // SUB)
                    rows = pl.ds(pl.multiple_of(first + r * SUB, SUB), SUB)
                    part = roll_lanes((sx, sy, sz_acc)[f][i, rows, :], sz.own * q - sz.halo)
                    tile = part if tile is None else jnp.where(lane < sz.own * q, tile, part)
                at = pl.multiple_of((p * sz.grad_tiles + g) * SUB, SUB)
                grads_out[key, dest, pl.ds(at, SUB), :] = tile
        return c

    lax.fori_loop(0, nx, write_grads, 0)


def packed(v):
    lane = lane_of((SUB, LANES))
    row = row_of((SUB, LANES))
    out = []
    for n in range(v.shape[0] // (4 * SUB)):
        tile = None
        for q in range(4):
            part = v[(4 * n + q) * SUB : (4 * n + q + 1) * SUB]
            keep = (lane % 2) + 2 * (row % 2)
            tile = part if tile is None else jnp.where(keep == q, part, tile)
        out.append(tile)
    return jnp.concatenate(out, axis=0)


def unpacked(v):
    lane = lane_of((SUB, LANES))
    row = row_of((SUB, LANES))
    out = []
    for n in range(v.shape[0] // SUB):
        tile = v[n * SUB : (n + 1) * SUB]
        for q in range(4):
            part = jnp.where(lane % 2 == q % 2, tile, z_up(tile) if q % 2 else z_down(tile))
            low = q // 2
            turned = pltpu.roll(part, SUB - 1 if low else 1, 0)
            out.append(jnp.where(row % 2 == low, part, turned))
    return jnp.concatenate(out, axis=0)


def rough_kernel(sz, start_ref, out_ref):
    for s in range(sz.space):
        for p in range(sz.planes):
            out_ref[s * sz.planes + p] = packed(averaged(start_ref[s, p * sz.ny : (p + 1) * sz.ny, :]))


def coarse_kernel(sz, *refs):
    pieces = refs[: sz.spans]
    jumps_ref, end_ref, out_ref = refs[sz.spans : sz.spans + 3]
    faces, coef, state, source = refs[sz.spans + 3 :]
    nx, ny = sz.nx, sz.ny
    body = slice(PAD, PAD + ny)
    turn = lax.axis_index("tm")
    lay_out_faces(sz, pieces, faces)
    for n in range(COARSE_SWEEPS + 1):
        clear_rim(state, (n,), nx, ny)
    valid = valid_columns(sz)

    def restricted(i, c):
        faces[0, i] = averaged(faces[0, i])
        faces[1, i] = 0.25 * averaged(faces[1, i])
        faces[2, i] = 0.25 * averaged(faces[2, i])
        faces[3, i] = averaged(faces[3, i])
        return c

    lax.fori_loop(0, nx, restricted, 0)

    def normalise(i, c):
        fx, fy, fz, cap = (faces[f, i] for f in range(4))
        bx = jnp.where(i == 0, 0.0, faces[0, jnp.maximum(i - 1, 0)])
        by, bz = row_down(fy, 2), z_down(fz, 2)
        diagonal = cap + COARSE_STEP * (fx + bx + fy + by + fz + bz)
        inv = jnp.where(valid, 1.0 / diagonal, 0.0)
        scaled = COARSE_STEP * inv
        for n, face in enumerate((fx, bx, fy, by, fz, bz)):
            coef[n, i] = face * scaled
        coef[6, i] = cap * inv
        return c

    lax.fori_loop(0, nx, normalise, 0)

    lane = lane_of((jumps_ref.shape[2], LANES))
    mine = (lane >= sz.halo) & (lane < sz.halo + sz.own)

    def squares(i, c):
        for k in range(sz.spans - 1):
            jump = jnp.where(mine, jumps_ref[k, i], 0.0)
            c = c + jump * jump
        return c

    square = lax.fori_loop(0, nx, squares, jnp.zeros((jumps_ref.shape[2], LANES), jnp.float32))
    square = functools.reduce(lambda a, b: a + b, [square[n : n + SUB] for n in range(0, square.shape[0], SUB)])

    def begin(i, c):
        state[0, i + 1, body, :] = jnp.zeros((ny, LANES), jnp.float32)
        state[COARSE_SWEEPS, i + 1, body, :] = jnp.zeros((ny, LANES), jnp.float32)
        return c

    lax.fori_loop(0, nx, begin, 0)

    for d in reversed(range(1, sz.spans)):
        which = jnp.maximum(turn - d, 0)
        there = turn >= d

        def take(i, c):
            jump = jnp.where(there, unpacked(jumps_ref[which, i]), 0.0)
            now = state[COARSE_SWEEPS, i + 1, body, :] + jump
            state[0, i + 1, body, :] = now
            source[i] = coef[6, i] * now
            return c

        lax.fori_loop(0, nx, take, 0)
        for n in range(COARSE_SWEEPS):

            def plane(i, c):
                v = state[n, i + 1, body, :]
                result = source[i] + coef[0, i] * state[n, i + 2, body, :] + coef[1, i] * state[n, i, body, :]
                result = result + coef[2, i] * state[n, i + 1, PAD + 2 : PAD + 2 + ny, :]
                result = result + coef[3, i] * state[n, i + 1, PAD - 2 : PAD - 2 + ny, :]
                result = result + coef[4, i] * z_up(v, 2) + coef[5, i] * z_down(v, 2)
                state[n + 1, i + 1, body, :] = result
                return c

            lax.fori_loop(0, nx, plane, 0)

    lane = lane_of((SUB, LANES))

    def write(i, c):
        dest, p = i // sz.planes, i % sz.planes
        result = state[COARSE_SWEEPS, i + 1, body, :] + end_ref[i]
        for g in range(sz.end_tiles):
            tile = None
            for q in range(sz.factor):
                n = g * sz.factor + q
                part = roll_lanes(result[n * SUB : (n + 1) * SUB], sz.own * q - sz.halo)
                tile = part if tile is None else jnp.where(lane < sz.own * q, tile, part)
            at = pl.multiple_of((p * sz.end_tiles + g) * SUB, SUB)
            out_ref[dest, pl.ds(at, SUB), :] = tile
        return c

    lax.fori_loop(0, nx, write, 0)
    for s in range(sz.space):
        out_ref[s, sz.end_rows : sz.end_rows + SUB, :] = square


def join_kernel(sz, kept_ref, come_ref, ends_ref, out_ref):
    for s in range(sz.space):
        out_ref[s, : sz.grad_rows, :] = kept_ref[0, s] + come_ref[0, s]
        out_ref[s, sz.grad_rows :, :] = ends_ref[s]


def unpack_kernel(sz, in_ref, ends_out, gx_out, gy_out, gz_out, norm_out):
    lane = lane_of((SUB, LANES))

    def whole_tile(tile, row, slot):
        result = None
        for q in range(sz.factor):
            block = tile * sz.factor + q
            part = roll_lanes(in_ref[block, row : row + SUB, :], sz.own * (q - slot))
            result = part if result is None else jnp.where(lane < sz.own * q, result, part)
        return result

    for t in range(sz.nz // LANES):
        columns = slice(t * LANES, (t + 1) * LANES)
        for p in range(sz.planes):
            for n in range(sz.grad_parts):
                f, r = divmod(n, sz.quarter // SUB)
                row = (p * sz.grad_tiles + n // sz.factor) * SUB
                (gx_out, gy_out, gz_out)[f][p, r * SUB : (r + 1) * SUB, columns] = whole_tile(t, row, n % sz.factor)
            for n in range(sz.end_parts):
                row = sz.grad_rows + (p * sz.end_tiles + n // sz.factor) * SUB
                ends_out[0, p, n * SUB : (n + 1) * SUB, columns] = whole_tile(t, row, n % sz.factor)
    squares = in_ref[0, sz.grad_rows + sz.end_rows :, :]
    for s in range(1, sz.space):
        squares = squares + in_ref[s, sz.grad_rows + sz.end_rows :, :]
    cells = (sz.spans - 1) * sz.nx * (sz.ny // 2) * (sz.nz // 2)
    whole = jnp.sum(jnp.sum(squares, axis=1, keepdims=True), axis=0, keepdims=True)
    norm_out[...] = jnp.sqrt(jnp.broadcast_to(whole, (SUB, LANES)) / cells)


def f32(*shape):
    return jax.ShapeDtypeStruct(shape, jnp.float32)


def call(kernel, sz, outs, scratch, *args, name):
    return pl.pallas_call(
        functools.partial(kernel, sz),
        out_shape=outs,
        scratch_shapes=[pltpu.VMEM(shape, jnp.float32) for shape in scratch],
        compiler_params=pltpu.CompilerParams(vmem_limit_bytes=VMEM_BYTES),
        name=name,
    )(*args)


def exchange(values, axis, bit):
    size = lax.axis_size(axis)
    return lax.ppermute(values, axis, [(i, i ^ bit) for i in range(size)])


def shards(start_states, diff_x, diff_y, diff_z, stress, trap_class, cotangent):
    spans, space = lax.axis_size("tm"), lax.axis_size("space")
    sz = Sizes(spans, space, *diff_x.shape)
    nx, ny = sz.nx, sz.ny
    part = f32(space, sz.planes * ny, LANES)
    coef, start, cot = call(
        windows_kernel,
        sz,
        (f32(space, 4 * sz.planes * sz.quarter, LANES), part, part),
        (),
        start_states,
        diff_x,
        diff_y,
        diff_z,
        stress,
        trap_class,
        cotangent,
        name="windows",
    )
    coef = lax.all_to_all(coef, "space", 0, 0)
    start = lax.all_to_all(start, "space", 0, 0)
    cot = lax.all_to_all(cot, "space", 0, 0)

    pieces = {0: coef}
    bit = spans // 2
    while bit:
        for key, piece in list(pieces.items()):
            pieces[key | bit] = exchange(piece, "tm", bit)
        bit //= 2
    pieces = [pieces[key] for key in range(spans)]

    rough = call(rough_kernel, sz, f32(nx, ny // 4, LANES), (), start, name="rough")
    following = lax.ppermute(rough, "tm", [(i + 1, i) for i in range(spans - 1)])

    padded = (nx + 2, ny + 2 * PAD, LANES)
    field = (nx, ny, LANES)
    end, rough_end, grads = call(
        fine_kernel,
        sz,
        (f32(*field), f32(nx, ny // 4, LANES), f32(spans, space, sz.grad_rows, LANES)),
        ((4,) + field, (8,) + field, (TOTAL + 1,) + padded, (2,) + padded)
        + (field, field, field, field, field, padded),
        *pieces,
        start,
        cot,
        name="fine",
    )

    jumps = jnp.where(lax.axis_index("tm") == spans - 1, 0.0, rough_end - following)
    jumps = lax.all_gather(jumps, "tm", axis=0)

    bit = spans // 2
    while bit:
        come = exchange(grads[bit:], "tm", bit)
        kept = grads[:bit]
        grads = kept + come if bit > 1 else None
        bit //= 2

    ends = call(
        coarse_kernel,
        sz,
        f32(space, sz.end_rows + SUB, LANES),
        ((4,) + field, (7,) + field, (COARSE_SWEEPS + 1,) + padded, field),
        *pieces,
        jumps,
        end,
        name="coarse",
    )
    joined = call(join_kernel, sz, f32(space, sz.out_rows, LANES), (), kept, come, ends, name="join")
    joined = lax.all_to_all(joined, "space", 0, 0)
    quarter = f32(sz.planes, sz.quarter, sz.nz)
    new_end, gx, gy, gz, norm = call(
        unpack_kernel,
        sz,
        (f32(1, sz.planes, ny, sz.nz), quarter, quarter, quarter, f32(SUB, LANES)),
        (),
        joined,
        name="unpack",
    )
    return new_end, gx, gy, gz, norm[0, 0]


def solution(mesh):
    fields = P("tm", "space", None, None)
    faces = P("space", None, None)
    quarter = P("space", "tm", None)
    return jax.shard_map(
        shards,
        mesh=mesh,
        in_specs=(fields, faces, faces, faces, faces, faces, fields),
        out_specs=(fields, quarter, quarter, quarter, P()),
        check_vma=False,
    )
```

```python
import functools
import math

import jax
import jax.numpy as jnp
from jax import lax
from jax.experimental import pallas as pl
from jax.experimental.pallas import tpu as pltpu
from jax.sharding import PartitionSpec as P

FINE_STEPS = 2
SWEEPS = 8
COARSE_SWEEPS = 2
TOTAL = FINE_STEPS * SWEEPS
LANES = 128
SUB = 8

STRESS_COUPLING = 0.5
TIME_STEP = 1.0
COARSE_STEP = FINE_STEPS * TIME_STEP
TRAP_LEVELS = (0.0, 1.0, 3.0, 7.0)

SPARE_BYTES = 2 * 1024 * 1024


class Sizes:
    def __init__(self, spans, space, planes, ny, nz):
        self.spans = spans
        self.space = space
        self.planes = planes
        self.nx = planes * space
        self.ny = ny
        self.nz = nz
        self.own = nz // space
        self.halo = (LANES - self.own) // 2
        self.quarter = ny // spans
        self.share = self.quarter // SUB
        self.tiles = ny // SUB
        self.factor = LANES // self.own
        self.grad_parts = 3 * self.share
        self.grad_tiles = -(-self.grad_parts // self.factor)
        self.end_parts = self.tiles
        self.end_tiles = self.end_parts // self.factor
        self.grad_rows = planes * self.grad_tiles * SUB
        self.end_rows = planes * self.end_tiles * SUB
        self.out_rows = self.grad_rows + self.end_rows + SUB
        assert self.tiles == SUB
        assert TOTAL + 2 * COARSE_SWEEPS * (spans - 1) <= self.halo


def lane_of(shape):
    return lax.broadcasted_iota(jnp.int32, shape, len(shape) - 1)


def row_of(shape):
    return lax.broadcasted_iota(jnp.int32, shape, len(shape) - 2)


def z_up(v, by=1):
    return pltpu.roll(v, LANES - by, v.ndim - 1)


def z_down(v, by=1):
    return pltpu.roll(v, by, v.ndim - 1)


def roll_lanes(v, by):
    by = by % LANES
    return v if by == 0 else pltpu.roll(v, by, 1)


def windows_kernel(sz, *refs):
    coef_out, field_out, columns = refs[7:10]
    start_ref, fx_ref, fy_ref, fz_ref, stress_ref, trap_ref, cot_ref = refs[10:17]
    copies = [pltpu.make_async_copy(refs[n], refs[10 + n], refs[17].at[n]) for n in range(7)]
    for n in (1, 2, 3, 4, 5, 0, 6):
        copies[n].start()
    for n in (1, 2, 3, 4, 5):
        copies[n].wait()
    turn = lax.axis_index("tm")
    count = sz.nz // LANES
    lane = lane_of((SUB, LANES))
    zero = jnp.zeros((SUB, LANES), jnp.float32)

    def cut(parts, out_ref, rows):
        for j in range(sz.space):
            first = sz.own * j - sz.halo
            tile, shift = first // LANES, first % LANES
            low = parts[tile] if 0 <= tile < count else zero
            if shift:
                high = parts[tile + 1] if tile + 1 < count else zero
                low = roll_lanes(jnp.where(lane < shift, high, low), -shift)
            out_ref[j, rows, :] = low

    for p in range(sz.planes):
        for n in range(count):
            cells = slice(n * LANES, (n + 1) * LANES)
            for f, ref in enumerate((fx_ref, fy_ref, fz_ref)):
                columns[f, p, n] = ref[p, :, cells]
            trap = trap_ref[p, :, cells]
            level = jnp.zeros(trap.shape, jnp.float32)
            for position, value in enumerate(TRAP_LEVELS):
                level = level + jnp.where(trap == position, value, 0.0)
            columns[3, p, n] = (1.0 + level) * jnp.exp(STRESS_COUPLING * stress_ref[p, :, cells])
        for f in range(4):
            for a in range(sz.share):
                rows = pl.ds(turn * sz.share + a, SUB, stride=sz.tiles)
                row = ((f * sz.planes + p) * sz.share + a) * SUB
                cut([columns[f, p, n, rows, :] for n in range(count)], coef_out, slice(row, row + SUB))
    for f, ref in enumerate((start_ref, cot_ref)):
        copies[6 * f].wait()
        for p in range(sz.planes):
            for r in range(SUB):
                parts = [
                    ref[0, p, r * sz.tiles : (r + 1) * sz.tiles, n * LANES : (n + 1) * LANES] for n in range(count)
                ]
                cut(parts, field_out, pl.ds((f * sz.planes + p) * sz.ny + r, sz.tiles, stride=SUB))


def valid_columns(sz):
    column = lax.axis_index("space") * sz.own - sz.halo + lane_of((SUB, LANES))
    return (column >= 0) & (column < sz.nz)


def lay_out_faces(sz, pieces, faces):
    turn = lax.axis_index("tm")
    for key, piece in enumerate(pieces):
        for f in range(4):
            for p in range(sz.planes):
                for a in range(sz.share):
                    row = ((f * sz.planes + p) * sz.share + a) * SUB
                    for s in range(sz.space):
                        faces[f, s * sz.planes + p, (turn ^ key) * sz.share + a] = piece[s, row : row + SUB, :]


def next_sublane(v):
    return jnp.where(row_of(v.shape) == SUB - 1, 0.0, pltpu.roll(v, SUB - 1, v.ndim - 2))


def last_sublane(v):
    return jnp.where(row_of(v.shape) == 0, 0.0, pltpu.roll(v, 1, v.ndim - 2))


def normalise(sz, faces, coef, count, step, apart):
    valid = valid_columns(sz)

    def one(i):
        for t in range(count):
            fx, fy, fz, cap = (faces[f, i, t] for f in range(4))
            bx = jnp.where(i == 0, 0.0, faces[0, jnp.maximum(i - 1, 0), t])
            by = faces[1, i, t - 1] if t else last_sublane(faces[1, i, count - 1])
            bz = z_down(fz, apart)
            diagonal = cap + step * (fx + bx + fy + by + fz + bz)
            inv = jnp.where(valid, 1.0 / diagonal, 0.0)
            scaled = step * inv
            for n, face in enumerate((fx, bx, fy, by, fz, bz)):
                coef[n, i, t] = face * scaled
            faces[2, i, t] = cap * inv
            faces[3, i, t] = inv

    def some(g, c):
        for q in range(4):
            one(4 * g + q)
        return c

    lax.fori_loop(0, sz.nx // 4, some, 0)


def store_plane(ref, at, v, count):
    ref[at, 0] = last_sublane(v[count - 1])
    ref[at, 1 : count + 1] = v
    ref[at, count + 1] = next_sublane(v[0])


def sweep(sz, coef, now, later, count, apart, source=None, kept=None):
    for i in range(sz.nx):
        v = now[i, 1 : count + 1]
        result = coef[2, i] * now[i, 2 : count + 2] + coef[3, i] * now[i, 0:count]
        result = result + coef[4, i] * z_up(v, apart) + coef[5, i] * z_down(v, apart)
        if i + 1 < sz.nx:
            result = result + coef[0, i] * now[i + 1, 1 : count + 1]
        if i:
            result = result + coef[1, i] * now[i - 1, 1 : count + 1]
        if source is not None:
            result = result + source[i]
        store_plane(later, i, result, count)
        if kept is not None:
            keep_plane(kept[0], kept[1], i, result, count)


def keep_plane(ref, k, i, v, count):
    ref[k, i, 0:count] = v
    ref[k, i, count] = next_sublane(v[0])


def coarse_rows(tile_of, m):
    v = tile_of(2 * m) + tile_of(2 * m + 1)
    return 0.25 * (v + jnp.where(lane_of(v.shape) % 2 == 0, z_up(v), z_down(v)))


def packed(low, high):
    return jnp.where(lane_of(low.shape) % 2 == 0, low, high)


def unpacked(v):
    even = lane_of(v.shape) % 2 == 0
    return jnp.where(even, v, z_down(v)), jnp.where(even, z_up(v), v)


def pack_rough(sz, tile_of):
    return [packed(coarse_rows(tile_of, 2 * m), coarse_rows(tile_of, 2 * m + 1)) for m in range(sz.tiles // 4)]


def fine_kernel(sz, *refs):
    pieces = refs[: sz.spans]
    field_ref, end_out, rough_out, grads_out = refs[sz.spans : sz.spans + 4]
    faces, coef, even, odd, source, fields, weights = refs[sz.spans + 4 :]
    nx, count = sz.nx, sz.tiles
    body = slice(1, count + 1)
    turn = lax.axis_index("tm")

    lay_out_faces(sz, pieces, faces)
    normalise(sz, faces, coef, count, TIME_STEP, 1)

    rim = jnp.zeros((count + 1, SUB, LANES), jnp.float32)
    for k in range(TOTAL + 1):
        fields[k, nx] = rim
        if k:
            weights[k - 1, nx] = rim

    def whole_plane(f, i):
        s, p = divmod(i, sz.planes)
        row = (f * sz.planes + p) * sz.ny
        return field_ref[s, row : row + sz.ny, :].reshape(count, SUB, LANES)

    for i in range(nx):
        v = whole_plane(0, i)
        store_plane(even, i, v, count)
        keep_plane(fields, 0, i, v, count)
    for step in range(FINE_STEPS):
        base = step * SWEEPS
        for i in range(nx):
            source[i] = faces[2, i] * even[i, body]

        def two(n, c):
            k = base + 2 * n
            sweep(sz, coef, even, odd, count, 1, source, (fields, k + 1))
            sweep(sz, coef, odd, even, count, 1, source, (fields, k + 2))
            return c

        lax.fori_loop(0, SWEEPS // 2, two, 0)

    for i in range(nx):
        end_out[i] = even[i, body]
        for m, rough in enumerate(pack_rough(sz, lambda t: even[i, 1 + t])):
            rough_out[i, m] = rough

    for i in range(nx):
        v = faces[3, i] * whole_plane(1, i)
        store_plane(even, i, v, count)
        keep_plane(weights, TOTAL - 1, i, v, count)
    for step in reversed(range(FINE_STEPS)):
        base = step * SWEEPS

        def two_back(n, c):
            k = base + SWEEPS - 1 - 2 * n
            sweep(sz, coef, even, odd, count, 1, None, (weights, k - 1))
            sweep(sz, coef, odd, even, count, 1, None, (weights, k - 2))
            return c

        lax.fori_loop(0, SWEEPS // 2 - 1, two_back, 0)
        sweep(sz, coef, even, odd, count, 1, None, (weights, base))
        if step:
            sweep(sz, coef, odd, even, count, 1, None)
            for i in range(nx):
                total = weights[base, i, 0:count]
                for k in range(base + 1, base + SWEEPS):
                    total = total + weights[k, i, 0:count]
                v = even[i, body] + faces[2, i] * total
                store_plane(odd, i, v, count)
                keep_plane(weights, base - 1, i, v, count)
            for i in range(nx):
                even[i] = odd[i]

    def gather_sums(i, c):
        for t in range(count):
            along = [None, None, None]
            whole = None
            for k in range(TOTAL):
                w, u = weights[k, i, t], fields[k, i, t]
                for d, (up_w, up_u) in enumerate(
                    (
                        (weights[k, i + 1, t], fields[k, i + 1, t]),
                        (weights[k, i, t + 1], fields[k, i, t + 1]),
                        (z_up(w), z_up(u)),
                    )
                ):
                    term = w * up_u + up_w * u
                    along[d] = term if along[d] is None else along[d] + term
                term = w * fields[k + 1, i, t]
                whole = term if whole is None else whole + term
            for d in range(3):
                faces[d, i, t] = along[d]
            even[i, t] = whole
            if t == 0:
                even[i, count] = next_sublane(whole)
        return c

    lax.fori_loop(0, nx, gather_sums, 0)
    rows = weights.reshape(TOTAL, nx + 1, (count + 1) * SUB, LANES)

    for i in range(nx):
        for t in range(count):
            here = even[i, t]
            for d, there in enumerate((even[i + 1, t] if i + 1 < nx else None, even[i, t + 1], z_up(here))):
                value = faces[d, i, t] - here
                if there is not None:
                    value = value - there
                rows[d, i, pl.ds(t, SUB, stride=count), :] = TIME_STEP * value

    lane = lane_of((SUB, LANES))
    for key in range(sz.spans):
        first = (turn ^ key) * sz.quarter
        for i in range(nx):
            dest, p = divmod(i, sz.planes)
            for g in range(sz.grad_tiles):
                tile = None
                for q in range(sz.factor):
                    n = g * sz.factor + q
                    if n >= sz.grad_parts:
                        continue
                    f, r = divmod(n, sz.share)
                    at = pl.ds(pl.multiple_of(first + r * SUB, SUB), SUB)
                    part = roll_lanes(rows[f, i, at, :], sz.own * q - sz.halo)
                    tile = part if tile is None else jnp.where(lane < sz.own * q, tile, part)
                row = (p * sz.grad_tiles + g) * SUB
                grads_out[key, dest, row : row + SUB, :] = tile


def rough_kernel(sz, start_ref, out_ref):
    for i in range(sz.nx):
        s, p = divmod(i, sz.planes)
        tile_of = lambda t: start_ref[s, (p * sz.tiles + t) * SUB : (p * sz.tiles + t + 1) * SUB, :]
        for m, rough in enumerate(pack_rough(sz, tile_of)):
            out_ref[i, m] = rough


def coarse_kernel(sz, *refs):
    pieces = refs[: sz.spans]
    jumps_ref, end_ref, out_ref = refs[sz.spans : sz.spans + 3]
    faces, rough, coef, even, odd, source = refs[sz.spans + 3 :]
    nx, count = sz.nx, sz.tiles // 2
    body = slice(1, count + 1)
    turn = lax.axis_index("tm")
    lay_out_faces(sz, pieces, faces)
    for i in range(nx):
        for f, scale in enumerate((1.0, 0.25, 0.25, 1.0)):
            for m in range(count):
                v = coarse_rows(lambda t: faces[f, i, t], m)
                rough[f, i, m] = v if scale == 1.0 else scale * v
    normalise(sz, rough, coef, count, COARSE_STEP, 2)

    lane = lane_of((SUB, LANES))
    mine = (lane >= sz.halo) & (lane < sz.halo + sz.own)
    square = jnp.zeros((SUB, LANES), jnp.float32)
    for k in range(sz.spans - 1):
        for i in range(nx):
            for m in range(count // 2):
                square = square + jumps_ref[k, i, m] * jumps_ref[k, i, m]
    square = jnp.where(mine, square, 0.0)

    for d in reversed(range(1, sz.spans)):
        which = jnp.maximum(turn - d, 0)
        there = turn >= d
        for i in range(nx):
            jump = []
            for m in range(count // 2):
                jump += unpacked(jnp.where(there, jumps_ref[which, i, m], 0.0))
            v = jnp.stack(jump)
            if d < sz.spans - 1:
                v = v + even[i, body]
            store_plane(even, i, v, count)
            source[i] = rough[2, i] * v
        for n in range(COARSE_SWEEPS // 2):
            sweep(sz, coef, even, odd, count, 2, source)
            sweep(sz, coef, odd, even, count, 2, source)

    for i in range(nx):
        dest, p = divmod(i, sz.planes)
        for g in range(sz.end_tiles):
            tile = None
            for q in range(sz.factor):
                n = g * sz.factor + q
                part = roll_lanes(end_ref[i, n] + even[i, 1 + n // 2], sz.own * q - sz.halo)
                tile = part if tile is None else jnp.where(lane < sz.own * q, tile, part)
            row = (p * sz.end_tiles + g) * SUB
            out_ref[dest, row : row + SUB, :] = tile
    for s in range(sz.space):
        out_ref[s, sz.end_rows : sz.end_rows + SUB, :] = square


def join_kernel(sz, kept_ref, come_ref, ends_ref, out_ref):
    for s in range(sz.space):
        out_ref[s, : sz.grad_rows, :] = kept_ref[0, s] + come_ref[0, s]
        out_ref[s, sz.grad_rows :, :] = ends_ref[s]


def unpack_kernel(sz, in_ref, ends_out, gx_out, gy_out, gz_out, norm_out, rows):
    lane = lane_of((SUB, LANES))

    def whole_tile(tile, row, slot):
        result = None
        for q in range(sz.factor):
            block = tile * sz.factor + q
            part = roll_lanes(in_ref[block, row : row + SUB, :], sz.own * (q - slot))
            result = part if result is None else jnp.where(lane < sz.own * q, result, part)
        return result

    for t in range(sz.nz // LANES):
        columns = slice(t * LANES, (t + 1) * LANES)
        for p in range(sz.planes):
            for n in range(sz.grad_parts):
                f, r = divmod(n, sz.share)
                row = (p * sz.grad_tiles + n // sz.factor) * SUB
                (gx_out, gy_out, gz_out)[f][p, r * SUB : (r + 1) * SUB, columns] = whole_tile(t, row, n % sz.factor)
            for n in range(sz.end_parts):
                row = sz.grad_rows + (p * sz.end_tiles + n // sz.factor) * SUB
                rows[t, p, pl.ds(n, SUB, stride=sz.tiles), :] = whole_tile(t, row, n % sz.factor)
            ends_out[0, p, :, columns] = rows[t, p]
    squares = in_ref[0, sz.grad_rows + sz.end_rows :, :]
    for s in range(1, sz.space):
        squares = squares + in_ref[s, sz.grad_rows + sz.end_rows :, :]
    cells = (sz.spans - 1) * sz.nx * (sz.ny // 2) * (sz.nz // 2)
    whole = jnp.sum(jnp.sum(squares, axis=1, keepdims=True), axis=0, keepdims=True)
    norm_out[...] = jnp.sqrt(jnp.broadcast_to(whole, (SUB, LANES)) / cells)


def f32(*shape):
    return jax.ShapeDtypeStruct(shape, jnp.float32)


def call(kernel, sz, outs, scratch, *args, name):
    held = sum(4 * math.prod(shape) for shape in scratch)
    held += sum(4 * math.prod(array.shape) for array in jax.tree.leaves((outs, args)))
    return pl.pallas_call(
        functools.partial(kernel, sz),
        out_shape=outs,
        scratch_shapes=[pltpu.VMEM(shape, jnp.float32) for shape in scratch],
        compiler_params=pltpu.CompilerParams(vmem_limit_bytes=held + SPARE_BYTES),
        name=name,
    )(*args)


def exchange(values, axis, bit):
    size = lax.axis_size(axis)
    return lax.ppermute(values, axis, [(i, i ^ bit) for i in range(size)])


def shards(start_states, diff_x, diff_y, diff_z, stress, trap_class, cotangent):
    spans, space = lax.axis_size("tm"), lax.axis_size("space")
    sz = Sizes(spans, space, *diff_x.shape)
    nx, ny = sz.nx, sz.ny
    inputs = (start_states, diff_x, diff_y, diff_z, stress, trap_class, cotangent)
    coef, both = pl.pallas_call(
        functools.partial(windows_kernel, sz),
        out_shape=(f32(space, 4 * sz.planes * sz.quarter, LANES), f32(space, 2 * sz.planes * ny, LANES)),
        in_specs=[pl.BlockSpec(memory_space=pltpu.HBM)] * len(inputs),
        scratch_shapes=[pltpu.VMEM((4, sz.planes, sz.nz // LANES, ny, LANES), jnp.float32)]
        + [pltpu.VMEM(array.shape, array.dtype) for array in inputs]
        + [pltpu.SemaphoreType.DMA((len(inputs),))],
        compiler_params=pltpu.CompilerParams(vmem_limit_bytes=60 * 1024 * 1024),
        name="windows",
    )(*inputs)
    coef = lax.all_to_all(coef, "space", 0, 0)
    both = lax.all_to_all(both, "space", 0, 0)

    pieces = {0: coef}
    bit = spans // 2
    while bit:
        for key, piece in list(pieces.items()):
            pieces[key | bit] = exchange(piece, "tm", bit)
        bit //= 2
    pieces = [pieces[key] for key in range(spans)]

    tiles = sz.tiles
    rough_shape = f32(nx, tiles // 4, SUB, LANES)
    rough = call(rough_kernel, sz, rough_shape, (), both, name="rough")
    following = lax.ppermute(rough, "tm", [(i + 1, i) for i in range(spans - 1)])

    def field(count, *front):
        return front + (count, SUB, LANES)

    both, rough = lax.optimization_barrier((both, rough))
    end, rough_end, grads = call(
        fine_kernel,
        sz,
        (f32(*field(tiles, nx)), rough_shape, f32(spans, space, sz.grad_rows, LANES)),
        (
            field(tiles, 4, nx),
            field(tiles, 6, nx),
            field(tiles + 2, nx),
            field(tiles + 2, nx),
            field(tiles, nx),
            field(tiles + 1, TOTAL + 1, nx + 1),
            field(tiles + 1, TOTAL, nx + 1),
        ),
        *pieces,
        both,
        name="fine",
    )
    jumps = jnp.where(lax.axis_index("tm") == spans - 1, 0.0, rough_end - following)
    jumps = lax.all_gather(jumps, "tm", axis=0)

    bit = spans // 2
    while bit:
        come = exchange(grads[bit:], "tm", bit)
        kept = grads[:bit]
        if bit == spans // 2:
            come, jumps = lax.optimization_barrier((come, jumps))
        grads = kept + come if bit > 1 else None
        bit //= 2

    ends = call(
        coarse_kernel,
        sz,
        f32(space, sz.end_rows + SUB, LANES),
        (
            field(tiles, 4, nx),
            field(tiles // 2, 4, nx),
            field(tiles // 2, 6, nx),
            field(tiles // 2 + 2, nx),
            field(tiles // 2 + 2, nx),
            field(tiles // 2, nx),
        ),
        *pieces,
        jumps,
        end,
        name="coarse",
    )
    joined = call(join_kernel, sz, f32(space, sz.out_rows, LANES), (), kept, come, ends, name="join")
    joined = lax.all_to_all(joined, "space", 0, 0)
    quarter = f32(sz.planes, sz.quarter, sz.nz)
    new_end, gx, gy, gz, norm = call(
        unpack_kernel,
        sz,
        (f32(1, sz.planes, ny, sz.nz), quarter, quarter, quarter, f32(SUB, LANES)),
        ((sz.nz // LANES, sz.planes, ny, LANES),),
        joined,
        name="unpack",
    )
    return new_end, gx, gy, gz, norm[0, 0]


def solution(mesh):
    fields = P("tm", "space", None, None)
    faces = P("space", None, None)
    quarter = P("space", "tm", None)
    return jax.shard_map(
        shards,
        mesh=mesh,
        in_specs=(fields, faces, faces, faces, faces, faces, fields),
        out_specs=(fields, quarter, quarter, quarter, P()),
        check_vma=False,
    )
```

```python
import functools
import math

import jax
import jax.numpy as jnp
from jax import lax
from jax.experimental import pallas as pl
from jax.experimental.pallas import tpu as pltpu
from jax.sharding import PartitionSpec as P

FINE_STEPS = 2
SWEEPS = 8
COARSE_SWEEPS = 2
TOTAL = FINE_STEPS * SWEEPS
LANES = 128
SUB = 8

STRESS_COUPLING = 0.5
TIME_STEP = 1.0
COARSE_STEP = FINE_STEPS * TIME_STEP
TRAP_LEVELS = (0.0, 1.0, 3.0, 7.0)

SPARE_BYTES = 2 * 1024 * 1024


class Sizes:
    def __init__(self, spans, space, planes, ny, nz):
        self.spans = spans
        self.space = space
        self.planes = planes
        self.nx = planes * space
        self.ny = ny
        self.nz = nz
        self.own = nz // space
        self.halo = (LANES - self.own) // 2
        self.quarter = ny // spans
        self.share = self.quarter // SUB
        self.tiles = ny // SUB
        self.factor = LANES // self.own
        self.grad_parts = 3 * self.share
        self.grad_tiles = -(-self.grad_parts // self.factor)
        self.end_parts = self.tiles
        self.end_tiles = self.end_parts // self.factor
        self.grad_rows = planes * self.grad_tiles * SUB
        self.end_rows = planes * self.end_tiles * SUB
        self.out_rows = self.grad_rows + self.end_rows + SUB
        self.reach = TOTAL
        self.width = self.own + 2 * self.reach
        self.spare = LANES - self.width
        self.mains = self.width // self.spare
        self.start_tiles = planes * self.tiles
        self.cot_tiles = planes * self.tiles * self.mains // (self.mains + 1)
        assert self.mains * self.spare == self.width and self.start_tiles % (self.mains + 1) == 0
        assert self.tiles == SUB
        assert TOTAL + 2 * COARSE_SWEEPS * (spans - 1) <= self.halo


def lane_of(shape):
    return lax.broadcasted_iota(jnp.int32, shape, len(shape) - 1)


def row_of(shape):
    return lax.broadcasted_iota(jnp.int32, shape, len(shape) - 2)


def z_up(v, by=1):
    return pltpu.roll(v, LANES - by, v.ndim - 1)


def z_down(v, by=1):
    return pltpu.roll(v, by, v.ndim - 1)


def roll_lanes(v, by):
    by = by % LANES
    return v if by == 0 else pltpu.roll(v, by, 1)


def windows_kernel(sz, *refs):
    coef_out, field_out, columns = refs[7:10]
    ordered = refs[18]
    start_ref, fx_ref, fy_ref, fz_ref, stress_ref, trap_ref, cot_ref = refs[10:17]
    copies = [pltpu.make_async_copy(refs[n], refs[10 + n], refs[17].at[n]) for n in range(7)]
    for n in (1, 2, 3, 4, 5, 0, 6):
        copies[n].start()
    for n in (1, 2, 3, 4, 5):
        copies[n].wait()
    turn = lax.axis_index("tm")
    count = sz.nz // LANES
    lane = lane_of((SUB, LANES))
    zero = jnp.zeros((SUB, LANES), jnp.float32)

    def window(parts, first):
        tile, shift = first // LANES, first % LANES
        low = parts[tile] if 0 <= tile < count else zero
        if shift:
            high = parts[tile + 1] if tile + 1 < count else zero
            low = roll_lanes(jnp.where(lane < shift, high, low), -shift)
        return low

    def cut(parts, out_ref, rows):
        for j in range(sz.space):
            out_ref[j, rows, :] = window(parts, sz.own * j - sz.halo)

    for p in range(sz.planes):
        for n in range(count):
            cells = slice(n * LANES, (n + 1) * LANES)
            for f, ref in enumerate((fx_ref, fy_ref, fz_ref)):
                columns[f, p, n] = ref[p, :, cells]
            trap = trap_ref[p, :, cells]
            level = jnp.zeros(trap.shape, jnp.float32)
            for position, value in enumerate(TRAP_LEVELS):
                level = level + jnp.where(trap == position, value, 0.0)
            columns[3, p, n] = (1.0 + level) * jnp.exp(STRESS_COUPLING * stress_ref[p, :, cells])
        for f in range(4):
            for a in range(sz.share):
                rows = pl.ds(turn * sz.share + a, SUB, stride=sz.tiles)
                row = ((f * sz.planes + p) * sz.share + a) * SUB
                cut([columns[f, p, n, rows, :] for n in range(count)], coef_out, slice(row, row + SUB))
    def tiled(ref, at):
        for p in range(sz.planes):
            for n in range(count):
                for r in range(SUB):
                    rows = slice(r * sz.tiles, (r + 1) * sz.tiles)
                    ordered[at, p, n, pl.ds(r, sz.tiles, stride=SUB), :] = ref[0, p, rows, n * LANES : (n + 1) * LANES]

    def tile_parts(at, q):
        p, t = divmod(q, sz.tiles)
        return [ordered[at, p, n, t * SUB : (t + 1) * SUB, :] for n in range(count)]

    copies[0].wait()
    tiled(start_ref, 0)
    for q in range(sz.start_tiles):
        cut(tile_parts(0, q), field_out, slice(q * SUB, (q + 1) * SUB))
    copies[6].wait()
    tiled(cot_ref, 1)
    for g in range(sz.cot_tiles // sz.mains):
        parts = [tile_parts(1, g * (sz.mains + 1) + q) for q in range(sz.mains + 1)]
        for j in range(sz.space):
            first = sz.own * j - sz.reach
            last = window(parts[sz.mains], first)
            for q in range(sz.mains):
                piece = roll_lanes(last, sz.width - sz.spare * q)
                row = (sz.start_tiles + g * sz.mains + q) * SUB
                field_out[j, row : row + SUB, :] = jnp.where(lane < sz.width, window(parts[q], first), piece)


def valid_columns(sz):
    column = lax.axis_index("space") * sz.own - sz.halo + lane_of((SUB, LANES))
    return (column >= 0) & (column < sz.nz)


def lay_out_faces(sz, pieces, faces):
    turn = lax.axis_index("tm")
    for key, piece in enumerate(pieces):
        for f in range(4):
            for p in range(sz.planes):
                for a in range(sz.share):
                    row = ((f * sz.planes + p) * sz.share + a) * SUB
                    for s in range(sz.space):
                        faces[f, s * sz.planes + p, (turn ^ key) * sz.share + a] = piece[s, row : row + SUB, :]


def next_sublane(v):
    return jnp.where(row_of(v.shape) == SUB - 1, 0.0, pltpu.roll(v, SUB - 1, v.ndim - 2))


def last_sublane(v):
    return jnp.where(row_of(v.shape) == 0, 0.0, pltpu.roll(v, 1, v.ndim - 2))


def normalise(sz, faces, coef, count, step, apart):
    valid = valid_columns(sz)

    def one(i):
        for t in range(count):
            fx, fy, fz, cap = (faces[f, i, t] for f in range(4))
            bx = jnp.where(i == 0, 0.0, faces[0, jnp.maximum(i - 1, 0), t])
            by = faces[1, i, t - 1] if t else last_sublane(faces[1, i, count - 1])
            bz = z_down(fz, apart)
            diagonal = cap + step * (fx + bx + fy + by + fz + bz)
            inv = jnp.where(valid, 1.0 / diagonal, 0.0)
            scaled = step * inv
            for n, face in enumerate((fx, bx, fy, by, fz, bz)):
                coef[n, i, t] = face * scaled
            faces[2, i, t] = cap * inv
            faces[3, i, t] = inv

    def some(g, c):
        for q in range(4):
            one(4 * g + q)
        return c

    lax.fori_loop(0, sz.nx // 4, some, 0)


def store_plane(ref, at, v, count):
    ref[at, 0] = last_sublane(v[count - 1])
    ref[at, 1 : count + 1] = v
    ref[at, count + 1] = next_sublane(v[0])


def sweep(sz, coef, now, later, count, apart, source=None, kept=None):
    for i in range(sz.nx):
        v = now[i, 1 : count + 1]
        result = coef[2, i] * now[i, 2 : count + 2] + coef[3, i] * now[i, 0:count]
        result = result + coef[4, i] * z_up(v, apart) + coef[5, i] * z_down(v, apart)
        if i + 1 < sz.nx:
            result = result + coef[0, i] * now[i + 1, 1 : count + 1]
        if i:
            result = result + coef[1, i] * now[i - 1, 1 : count + 1]
        if source is not None:
            result = result + source[i]
        store_plane(later, i, result, count)
        if kept is not None:
            keep_plane(kept[0], kept[1], i, result, count)


def keep_plane(ref, k, i, v, count):
    ref[k, i, 0:count] = v
    ref[k, i, count] = next_sublane(v[0])


def coarse_rows(tile_of, m):
    v = tile_of(2 * m) + tile_of(2 * m + 1)
    return 0.25 * (v + jnp.where(lane_of(v.shape) % 2 == 0, z_up(v), z_down(v)))


def packed(low, high):
    return jnp.where(lane_of(low.shape) % 2 == 0, low, high)


def unpacked(v):
    even = lane_of(v.shape) % 2 == 0
    return jnp.where(even, v, z_down(v)), jnp.where(even, z_up(v), v)


def pack_rough(sz, tile_of):
    return [packed(coarse_rows(tile_of, 2 * m), coarse_rows(tile_of, 2 * m + 1)) for m in range(sz.tiles // 4)]


def fine_kernel(sz, *refs):
    pieces = refs[: sz.spans]
    field_ref, end_out, rough_out, grads_out = refs[sz.spans : sz.spans + 4]
    faces, coef, even, odd, source, fields, weights = refs[sz.spans + 4 :]
    nx, count = sz.nx, sz.tiles
    body = slice(1, count + 1)
    turn = lax.axis_index("tm")

    lay_out_faces(sz, pieces, faces)
    normalise(sz, faces, coef, count, TIME_STEP, 1)

    rim = jnp.zeros((count + 1, SUB, LANES), jnp.float32)
    for k in range(TOTAL + 1):
        fields[k, nx] = rim
        if k:
            weights[k - 1, nx] = rim

    lane = lane_of((SUB, LANES))
    aside = sz.halo - sz.reach

    def start_plane(i):
        s, p = divmod(i, sz.planes)
        return field_ref[s, p * sz.ny : (p + 1) * sz.ny, :].reshape(count, SUB, LANES)

    def cot_tile(s, n):
        g, q = divmod(n, sz.mains + 1)
        mains = [sz.start_tiles + g * sz.mains + m for m in range(sz.mains)]
        main = lambda m: field_ref[s, mains[m] * SUB : (mains[m] + 1) * SUB, :]
        if q < sz.mains:
            return roll_lanes(main(q), aside)
        result = None
        for m in range(sz.mains):
            part = roll_lanes(main(m), sz.spare * m - sz.width + aside)
            result = part if result is None else jnp.where(lane < sz.spare * m + aside, result, part)
        return result

    def cot_plane(i):
        s, p = divmod(i, sz.planes)
        return jnp.stack([cot_tile(s, p * count + t) for t in range(count)])

    for i in range(nx):
        v = start_plane(i)
        store_plane(even, i, v, count)
        keep_plane(fields, 0, i, v, count)
    for step in range(FINE_STEPS):
        base = step * SWEEPS
        for i in range(nx):
            source[i] = faces[2, i] * even[i, body]

        def two(n, c):
            k = base + 2 * n
            sweep(sz, coef, even, odd, count, 1, source, (fields, k + 1))
            sweep(sz, coef, odd, even, count, 1, source, (fields, k + 2))
            return c

        lax.fori_loop(0, SWEEPS // 2, two, 0)

    for i in range(nx):
        end_out[i] = even[i, body]
        for m, rough in enumerate(pack_rough(sz, lambda t: even[i, 1 + t])):
            rough_out[i, m] = rough

    for i in range(nx):
        v = faces[3, i] * cot_plane(i)
        store_plane(even, i, v, count)
        keep_plane(weights, TOTAL - 1, i, v, count)
    for step in reversed(range(FINE_STEPS)):
        base = step * SWEEPS

        def two_back(n, c):
            k = base + SWEEPS - 1 - 2 * n
            sweep(sz, coef, even, odd, count, 1, None, (weights, k - 1))
            sweep(sz, coef, odd, even, count, 1, None, (weights, k - 2))
            return c

        lax.fori_loop(0, SWEEPS // 2 - 1, two_back, 0)
        sweep(sz, coef, even, odd, count, 1, None, (weights, base))
        if step:
            sweep(sz, coef, odd, even, count, 1, None)
            for i in range(nx):
                total = weights[base, i, 0:count]
                for k in range(base + 1, base + SWEEPS):
                    total = total + weights[k, i, 0:count]
                v = even[i, body] + faces[2, i] * total
                store_plane(odd, i, v, count)
                keep_plane(weights, base - 1, i, v, count)
            for i in range(nx):
                even[i] = odd[i]

    def gather_sums(i, c):
        for t in range(count):
            along = [None, None, None]
            whole = None
            for k in range(TOTAL):
                w, u = weights[k, i, t], fields[k, i, t]
                for d, (up_w, up_u) in enumerate(
                    (
                        (weights[k, i + 1, t], fields[k, i + 1, t]),
                        (weights[k, i, t + 1], fields[k, i, t + 1]),
                        (z_up(w), z_up(u)),
                    )
                ):
                    term = w * up_u + up_w * u
                    along[d] = term if along[d] is None else along[d] + term
                term = w * fields[k + 1, i, t]
                whole = term if whole is None else whole + term
            for d in range(3):
                faces[d, i, t] = along[d]
            even[i, t] = whole
            if t == 0:
                even[i, count] = next_sublane(whole)
        return c

    lax.fori_loop(0, nx, gather_sums, 0)
    rows = weights.reshape(TOTAL, nx + 1, (count + 1) * SUB, LANES)

    for i in range(nx):
        for t in range(count):
            here = even[i, t]
            for d, there in enumerate((even[i + 1, t] if i + 1 < nx else None, even[i, t + 1], z_up(here))):
                value = faces[d, i, t] - here
                if there is not None:
                    value = value - there
                rows[d, i, pl.ds(t, SUB, stride=count), :] = TIME_STEP * value

    for at in range(sz.spans):
        first = (turn ^ turned(at, sz.spans)) * sz.quarter
        for i in range(nx):
            dest, p = divmod(i, sz.planes)
            for g in range(sz.grad_tiles):
                tile = None
                for q in range(sz.factor):
                    n = g * sz.factor + q
                    if n >= sz.grad_parts:
                        continue
                    f, r = divmod(n, sz.share)
                    place = pl.ds(pl.multiple_of(first + r * SUB, SUB), SUB)
                    part = roll_lanes(rows[f, i, place, :], sz.own * q - sz.halo)
                    tile = part if tile is None else jnp.where(lane < sz.own * q, tile, part)
                row = (p * sz.grad_tiles + g) * SUB
                grads_out[at, dest, row : row + SUB, :] = tile


def rough_kernel(sz, start_ref, out_ref):
    for i in range(sz.nx):
        s, p = divmod(i, sz.planes)
        tile_of = lambda t: start_ref[s, (p * sz.tiles + t) * SUB : (p * sz.tiles + t + 1) * SUB, :]
        for m, rough in enumerate(pack_rough(sz, tile_of)):
            out_ref[i, m] = rough


def coarse_kernel(sz, *refs):
    pieces = refs[: sz.spans]
    jumps_ref, end_ref, out_ref = refs[sz.spans : sz.spans + 3]
    faces, rough, coef, even, odd, source = refs[sz.spans + 3 :]
    nx, count = sz.nx, sz.tiles // 2
    body = slice(1, count + 1)
    turn = lax.axis_index("tm")
    lay_out_faces(sz, pieces, faces)
    for i in range(nx):
        for f, scale in enumerate((1.0, 0.25, 0.25, 1.0)):
            for m in range(count):
                v = coarse_rows(lambda t: faces[f, i, t], m)
                rough[f, i, m] = v if scale == 1.0 else scale * v
    normalise(sz, rough, coef, count, COARSE_STEP, 2)

    lane = lane_of((SUB, LANES))
    mine = (lane >= sz.halo) & (lane < sz.halo + sz.own)
    square = jnp.zeros((SUB, LANES), jnp.float32)
    for k in range(sz.spans - 1):
        for i in range(nx):
            for m in range(count // 2):
                square = square + jumps_ref[k, i, m] * jumps_ref[k, i, m]
    square = jnp.where(mine, square, 0.0)

    for d in reversed(range(1, sz.spans)):
        which = jnp.maximum(turn - d, 0)
        there = turn >= d
        for i in range(nx):
            jump = []
            for m in range(count // 2):
                jump += unpacked(jnp.where(there, jumps_ref[which, i, m], 0.0))
            v = jnp.stack(jump)
            if d < sz.spans - 1:
                v = v + even[i, body]
            store_plane(even, i, v, count)
            source[i] = rough[2, i] * v
        for n in range(COARSE_SWEEPS // 2):
            sweep(sz, coef, even, odd, count, 2, source)
            sweep(sz, coef, odd, even, count, 2, source)

    for i in range(nx):
        dest, p = divmod(i, sz.planes)
        for g in range(sz.end_tiles):
            tile = None
            for q in range(sz.factor):
                n = g * sz.factor + q
                part = roll_lanes(end_ref[i, n] + even[i, 1 + n // 2], sz.own * q - sz.halo)
                tile = part if tile is None else jnp.where(lane < sz.own * q, tile, part)
            row = (p * sz.end_tiles + g) * SUB
            out_ref[dest, row : row + SUB, :] = tile
    for s in range(sz.space):
        out_ref[s, sz.end_rows : sz.end_rows + SUB, :] = square


def join_kernel(sz, kept_ref, come_ref, ends_ref, out_ref):
    for s in range(sz.space):
        out_ref[s, : sz.grad_rows, :] = kept_ref[0, s] + come_ref[0, s]
        out_ref[s, sz.grad_rows :, :] = ends_ref[s]


def unpack_kernel(sz, in_ref, ends_out, gx_out, gy_out, gz_out, norm_out, rows):
    lane = lane_of((SUB, LANES))

    def whole_tile(tile, row, slot):
        result = None
        for q in range(sz.factor):
            block = tile * sz.factor + q
            part = roll_lanes(in_ref[block, row : row + SUB, :], sz.own * (q - slot))
            result = part if result is None else jnp.where(lane < sz.own * q, result, part)
        return result

    for t in range(sz.nz // LANES):
        columns = slice(t * LANES, (t + 1) * LANES)
        for p in range(sz.planes):
            for n in range(sz.grad_parts):
                f, r = divmod(n, sz.share)
                row = (p * sz.grad_tiles + n // sz.factor) * SUB
                (gx_out, gy_out, gz_out)[f][p, r * SUB : (r + 1) * SUB, columns] = whole_tile(t, row, n % sz.factor)
            for n in range(sz.end_parts):
                row = sz.grad_rows + (p * sz.end_tiles + n // sz.factor) * SUB
                rows[t, p, pl.ds(n, SUB, stride=sz.tiles), :] = whole_tile(t, row, n % sz.factor)
            ends_out[0, p, :, columns] = rows[t, p]
    squares = in_ref[0, sz.grad_rows + sz.end_rows :, :]
    for s in range(1, sz.space):
        squares = squares + in_ref[s, sz.grad_rows + sz.end_rows :, :]
    cells = (sz.spans - 1) * sz.nx * (sz.ny // 2) * (sz.nz // 2)
    whole = jnp.sum(jnp.sum(squares, axis=1, keepdims=True), axis=0, keepdims=True)
    norm_out[...] = jnp.sqrt(whole / cells)


def f32(*shape):
    return jax.ShapeDtypeStruct(shape, jnp.float32)


def call(kernel, sz, outs, scratch, *args, name):
    held = sum(4 * math.prod(shape) for shape in scratch)
    held += sum(4 * math.prod(array.shape) for array in jax.tree.leaves((outs, args)))
    return pl.pallas_call(
        functools.partial(kernel, sz),
        out_shape=outs,
        scratch_shapes=[pltpu.VMEM(shape, jnp.float32) for shape in scratch],
        compiler_params=pltpu.CompilerParams(vmem_limit_bytes=held + SPARE_BYTES),
        name=name,
    )(*args)


def turned(index, size):
    result = 0
    while size > 1:
        result, index, size = result * 2 + index % 2, index // 2, size // 2
    return result


def exchange(values, axis, bit):
    size = lax.axis_size(axis)
    return lax.ppermute(values, axis, [(i, i ^ bit) for i in range(size)])


def shards(start_states, diff_x, diff_y, diff_z, stress, trap_class, cotangent):
    spans, space = lax.axis_size("tm"), lax.axis_size("space")
    sz = Sizes(spans, space, *diff_x.shape)
    nx, ny = sz.nx, sz.ny
    inputs = (start_states, diff_x, diff_y, diff_z, stress, trap_class, cotangent)
    coef, both = pl.pallas_call(
        functools.partial(windows_kernel, sz),
        out_shape=(f32(space, 4 * sz.planes * sz.quarter, LANES), f32(space, (sz.start_tiles + sz.cot_tiles) * SUB, LANES)),
        in_specs=[pl.BlockSpec(memory_space=pltpu.HBM)] * len(inputs),
        scratch_shapes=[pltpu.VMEM((4, sz.planes, sz.nz // LANES, ny, LANES), jnp.float32)]
        + [pltpu.VMEM(array.shape, array.dtype) for array in inputs]
        + [pltpu.SemaphoreType.DMA((len(inputs),))]
        + [pltpu.VMEM((2, sz.planes, sz.nz // LANES, ny, LANES), jnp.float32)],
        compiler_params=pltpu.CompilerParams(vmem_limit_bytes=60 * 1024 * 1024),
        name="windows",
    )(*inputs)
    coef = lax.all_to_all(coef, "space", 0, 0)
    both = lax.all_to_all(both, "space", 0, 0)

    pieces = {0: coef}
    bit = spans // 2
    while bit:
        for key, piece in list(pieces.items()):
            pieces[key | bit] = exchange(piece, "tm", bit)
        bit //= 2
    pieces = [pieces[key] for key in range(spans)]

    tiles = sz.tiles
    rough_shape = f32(nx, tiles // 4, SUB, LANES)
    rough = call(rough_kernel, sz, rough_shape, (), both, name="rough")
    following = lax.ppermute(rough, "tm", [(i + 1, i) for i in range(spans - 1)])

    def field(count, *front):
        return front + (count, SUB, LANES)

    both, rough = lax.optimization_barrier((both, rough))
    end, rough_end, grads = call(
        fine_kernel,
        sz,
        (f32(*field(tiles, nx)), rough_shape, f32(spans, space, sz.grad_rows, LANES)),
        (
            field(tiles, 4, nx),
            field(tiles, 6, nx),
            field(tiles + 2, nx),
            field(tiles + 2, nx),
            field(tiles, nx),
            field(tiles + 1, TOTAL + 1, nx + 1),
            field(tiles + 1, TOTAL, nx + 1),
        ),
        *pieces,
        both,
        name="fine",
    )
    jumps = jnp.where(lax.axis_index("tm") == spans - 1, 0.0, rough_end - following)
    jumps = lax.all_gather(jumps, "tm", axis=0)

    half, bit = spans // 2, 1
    while half:
        come = exchange(grads[half:], "tm", bit)
        kept = grads[:half]
        if bit == 1:
            come, jumps = lax.optimization_barrier((come, jumps))
        grads = kept + come if half > 1 else None
        half, bit = half // 2, bit * 2

    ends = call(
        coarse_kernel,
        sz,
        f32(space, sz.end_rows + SUB, LANES),
        (
            field(tiles, 4, nx),
            field(tiles // 2, 4, nx),
            field(tiles // 2, 6, nx),
            field(tiles // 2 + 2, nx),
            field(tiles // 2 + 2, nx),
            field(tiles // 2, nx),
        ),
        *pieces,
        jumps,
        end,
        name="coarse",
    )
    joined = call(join_kernel, sz, f32(space, sz.out_rows, LANES), (), kept, come, ends, name="join")
    joined = lax.all_to_all(joined, "space", 0, 0)
    quarter = f32(sz.planes, sz.quarter, sz.nz)
    new_end, gx, gy, gz, norm = call(
        unpack_kernel,
        sz,
        (f32(1, sz.planes, ny, sz.nz), quarter, quarter, quarter, f32(1, 1)),
        ((sz.nz // LANES, sz.planes, ny, LANES),),
        joined,
        name="unpack",
    )
    return new_end, gx, gy, gz, norm.reshape(())


def solution(mesh):
    fields = P("tm", "space", None, None)
    faces = P("space", None, None)
    quarter = P("space", "tm", None)
    return jax.shard_map(
        shards,
        mesh=mesh,
        in_specs=(fields, faces, faces, faces, faces, faces, fields),
        out_specs=(fields, quarter, quarter, quarter, P()),
        check_vma=False,
    )
```

```python
import functools
import math

import jax
import jax.numpy as jnp
from jax import lax
from jax.experimental import pallas as pl
from jax.experimental.pallas import tpu as pltpu
from jax.sharding import PartitionSpec as P

FINE_STEPS = 2
SWEEPS = 8
COARSE_SWEEPS = 2
TOTAL = FINE_STEPS * SWEEPS
LANES = 128
SUB = 8

STRESS_COUPLING = 0.5
TIME_STEP = 1.0
COARSE_STEP = FINE_STEPS * TIME_STEP
TRAP_LEVELS = (0.0, 1.0, 3.0, 7.0)

SPARE_BYTES = 3 * 512 * 1024


class Sizes:
    def __init__(self, spans, space, planes, ny, nz):
        self.spans = spans
        self.space = space
        self.planes = planes
        self.nx = planes * space
        self.ny = ny
        self.nz = nz
        self.own = nz // space
        self.halo = (LANES - self.own) // 2
        self.quarter = ny // spans
        self.share = self.quarter // SUB
        self.tiles = ny // SUB
        self.factor = LANES // self.own
        self.grad_parts = 3 * self.share
        self.grad_tiles = -(-self.grad_parts // self.factor)
        self.end_parts = self.tiles
        self.end_tiles = self.end_parts // self.factor
        self.grad_rows = planes * self.grad_tiles * SUB
        self.end_rows = planes * self.end_tiles * SUB
        self.out_rows = self.grad_rows + self.end_rows + SUB
        self.reach = TOTAL
        self.width = self.own + 2 * self.reach
        self.spare = LANES - self.width
        self.mains = self.width // self.spare
        self.start_tiles = planes * self.tiles
        self.cot_tiles = planes * self.tiles * self.mains // (self.mains + 1)
        assert self.mains * self.spare == self.width and self.start_tiles % (self.mains + 1) == 0
        assert self.tiles == SUB
        assert TOTAL + 2 * COARSE_SWEEPS * (spans - 1) <= self.halo


def lane_of(shape):
    return lax.broadcasted_iota(jnp.int32, shape, len(shape) - 1)


def row_of(shape):
    return lax.broadcasted_iota(jnp.int32, shape, len(shape) - 2)


def z_up(v, by=1):
    return pltpu.roll(v, LANES - by, v.ndim - 1)


def z_down(v, by=1):
    return pltpu.roll(v, by, v.ndim - 1)


def roll_lanes(v, by):
    by = by % LANES
    return v if by == 0 else pltpu.roll(v, by, 1)


def window(parts, first):
    lane = lane_of((SUB, LANES))
    zero = jnp.zeros((SUB, LANES), jnp.float32)
    tile, shift = first // LANES, first % LANES
    low = parts[tile] if 0 <= tile < len(parts) else zero
    if shift:
        high = parts[tile + 1] if tile + 1 < len(parts) else zero
        low = roll_lanes(jnp.where(lane < shift, high, low), -shift)
    return low


def start_copies(refs, count):
    copies = [pltpu.make_async_copy(refs[n], refs[count + 1 + n], refs[-1].at[n]) for n in range(count)]
    for copy in copies:
        copy.start()
    return copies


def face_windows_kernel(sz, *refs):
    fx_ref, fy_ref, fz_ref, stress_ref, trap_ref = refs[6:11]
    coef_out, columns = refs[5], refs[11]
    turn = lax.axis_index("tm")
    count = sz.nz // LANES
    copies = start_copies(refs, 5)

    def cut_field(f, p):
        for a in range(sz.share):
            rows = pl.ds(turn * sz.share + a, SUB, stride=sz.tiles)
            row = ((f * sz.planes + p) * sz.share + a) * SUB
            parts = [columns[f, p, n, rows, :] for n in range(count)]
            for j in range(sz.space):
                coef_out[j, row : row + SUB, :] = window(parts, sz.own * j - sz.halo)

    for f, ref in enumerate((fx_ref, fy_ref, fz_ref)):
        copies[f].wait()
        for p in range(sz.planes):
            for n in range(count):
                columns[f, p, n] = ref[p, :, n * LANES : (n + 1) * LANES]
            cut_field(f, p)
    copies[3].wait()
    copies[4].wait()
    for p in range(sz.planes):
        for n in range(count):
            cells = slice(n * LANES, (n + 1) * LANES)
            trap = trap_ref[p, :, cells]
            level = jnp.zeros(trap.shape, jnp.float32)
            for position, value in enumerate(TRAP_LEVELS):
                level = level + jnp.where(trap == position, value, 0.0)
            columns[3, p, n] = (1.0 + level) * jnp.exp(STRESS_COUPLING * stress_ref[p, :, cells])
        cut_field(3, p)


def field_windows_kernel(sz, *refs):
    start_ref, cot_ref = refs[3:5]
    field_out, ordered = refs[2], refs[5]
    count = sz.nz // LANES
    lane = lane_of((SUB, LANES))
    copies = start_copies(refs, 2)

    def tiled(ref, at):
        for p in range(sz.planes):
            for n in range(count):
                for r in range(SUB):
                    rows = slice(r * sz.tiles, (r + 1) * sz.tiles)
                    ordered[at, p, n, pl.ds(r, sz.tiles, stride=SUB), :] = ref[0, p, rows, n * LANES : (n + 1) * LANES]

    def tile_parts(at, q):
        p, t = divmod(q, sz.tiles)
        return [ordered[at, p, n, t * SUB : (t + 1) * SUB, :] for n in range(count)]

    copies[0].wait()
    tiled(start_ref, 0)
    for q in range(sz.start_tiles):
        parts = tile_parts(0, q)
        for j in range(sz.space):
            field_out[j, q * SUB : (q + 1) * SUB, :] = window(parts, sz.own * j - sz.halo)
    copies[1].wait()
    tiled(cot_ref, 1)
    for g in range(sz.cot_tiles // sz.mains):
        parts = [tile_parts(1, g * (sz.mains + 1) + q) for q in range(sz.mains + 1)]
        for j in range(sz.space):
            first = sz.own * j - sz.reach
            last = window(parts[sz.mains], first)
            for q in range(sz.mains):
                piece = roll_lanes(last, sz.width - sz.spare * q)
                row = (sz.start_tiles + g * sz.mains + q) * SUB
                field_out[j, row : row + SUB, :] = jnp.where(lane < sz.width, window(parts[q], first), piece)


def valid_columns(sz):
    column = lax.axis_index("space") * sz.own - sz.halo + lane_of((SUB, LANES))
    return (column >= 0) & (column < sz.nz)


def lay_out_faces(sz, pieces, faces):
    turn = lax.axis_index("tm")
    for key, piece in enumerate(pieces):
        for f in range(4):
            for p in range(sz.planes):
                for a in range(sz.share):
                    row = ((f * sz.planes + p) * sz.share + a) * SUB
                    for s in range(sz.space):
                        faces[f, s * sz.planes + p, (turn ^ key) * sz.share + a] = piece[s, row : row + SUB, :]


def next_sublane(v):
    return jnp.where(row_of(v.shape) == SUB - 1, 0.0, pltpu.roll(v, SUB - 1, v.ndim - 2))


def last_sublane(v):
    return jnp.where(row_of(v.shape) == 0, 0.0, pltpu.roll(v, 1, v.ndim - 2))


def normalise(sz, faces, coef, scale, count, step, apart):
    valid = valid_columns(sz)

    def one(i):
        for t in range(count):
            fx, fy, fz, cap = (faces[f, i, t] for f in range(4))
            bx = jnp.where(i == 0, 0.0, faces[0, jnp.maximum(i - 1, 0), t])
            by = faces[1, i, t - 1] if t else last_sublane(faces[1, i, count - 1])
            bz = z_down(fz, apart)
            diagonal = cap + step * (fx + bx + fy + by + fz + bz)
            inv = jnp.where(valid, 1.0 / diagonal, 0.0)
            scaled = step * inv
            for n, face in enumerate((fx, bx, fy, by, fz, bz)):
                coef[n, i, t] = face * scaled
            scale[0, i, t] = cap * inv
            scale[1, i, t] = inv

    def some(g, c):
        for q in range(4):
            one(4 * g + q)
        return c

    lax.fori_loop(0, sz.nx // 4, some, 0)


def store_plane(ref, at, v, count):
    ref[at, 0] = last_sublane(v[count - 1])
    ref[at, 1 : count + 1] = v
    ref[at, count + 1] = next_sublane(v[0])


def sweep(sz, coef, now, later, count, apart, source=None, kept=None):
    for i in range(sz.nx):
        v = now[i, 1 : count + 1]
        result = coef[2, i] * now[i, 2 : count + 2] + coef[3, i] * now[i, 0:count]
        result = result + coef[4, i] * z_up(v, apart) + coef[5, i] * z_down(v, apart)
        if i + 1 < sz.nx:
            result = result + coef[0, i] * now[i + 1, 1 : count + 1]
        if i:
            result = result + coef[1, i] * now[i - 1, 1 : count + 1]
        if source is not None:
            result = result + source[i]
        store_plane(later, i, result, count)
        if kept is not None:
            keep_plane(kept[0], kept[1], i, result, count)


def two_sweeps(sz, coef, count, source, forward, adjoint):
    for i in range(sz.nx):
        factors = [coef[n, i] for n in range(6)]
        for job in (forward, adjoint):
            if job is None:
                continue
            now, later, kept, at = job
            v = now[i, 1 : count + 1]
            result = factors[2] * now[i, 2 : count + 2] + factors[3] * now[i, 0:count]
            result = result + factors[4] * z_up(v) + factors[5] * z_down(v)
            if i + 1 < sz.nx:
                result = result + factors[0] * now[i + 1, 1 : count + 1]
            if i:
                result = result + factors[1] * now[i - 1, 1 : count + 1]
            if job is forward:
                result = result + source[0, i]
            store_plane(later, i, result, count)
            if kept is not None:
                keep_plane(kept, at, i, result, count)


def keep_plane(ref, k, i, v, count):
    ref[k, i, 0:count] = v
    ref[k, i, count] = next_sublane(v[0])


def coarse_rows(tile_of, m):
    v = tile_of(2 * m) + tile_of(2 * m + 1)
    return 0.25 * (v + jnp.where(lane_of(v.shape) % 2 == 0, z_up(v), z_down(v)))


def packed(low, high):
    return jnp.where(lane_of(low.shape) % 2 == 0, low, high)


def unpacked(v):
    even = lane_of(v.shape) % 2 == 0
    return jnp.where(even, v, z_down(v)), jnp.where(even, z_up(v), v)


def pack_rough(sz, tile_of):
    return [packed(coarse_rows(tile_of, 2 * m), coarse_rows(tile_of, 2 * m + 1)) for m in range(sz.tiles // 4)]


def factors_kernel(sz, *refs):
    pieces = refs[: sz.spans]
    coef_out, scale_out, faces = refs[sz.spans :]
    lay_out_faces(sz, pieces, faces)
    normalise(sz, faces, coef_out, scale_out, sz.tiles, TIME_STEP, 1)


def fine_kernel(sz, *refs):
    coef, scale, field_ref, end_out, rough_out, grads_out = refs[:6]
    sums, even, odd, back, forth, fields, weights = refs[6:]
    nx, count = sz.nx, sz.tiles
    body = slice(1, count + 1)
    turn = lax.axis_index("tm")

    rim = jnp.zeros((count + 1, SUB, LANES), jnp.float32)
    for k in range(TOTAL + 1):
        fields[k, nx] = rim
        if k:
            weights[k - 1, nx] = rim

    lane = lane_of((SUB, LANES))
    aside = sz.halo - sz.reach

    def start_plane(i):
        s, p = divmod(i, sz.planes)
        return field_ref[s, p * sz.ny : (p + 1) * sz.ny, :].reshape(count, SUB, LANES)

    def cot_tile(s, n):
        g, q = divmod(n, sz.mains + 1)
        mains = [sz.start_tiles + g * sz.mains + m for m in range(sz.mains)]
        main = lambda m: field_ref[s, mains[m] * SUB : (mains[m] + 1) * SUB, :]
        if q < sz.mains:
            return roll_lanes(main(q), aside)
        result = None
        for m in range(sz.mains):
            part = roll_lanes(main(m), sz.spare * m - sz.width + aside)
            result = part if result is None else jnp.where(lane < sz.spare * m + aside, result, part)
        return result

    def cot_plane(i):
        s, p = divmod(i, sz.planes)
        return jnp.stack([cot_tile(s, p * count + t) for t in range(count)])

    for i in range(nx):
        v = start_plane(i)
        store_plane(even, i, v, count)
        keep_plane(fields, 0, i, v, count)
        v = scale[1, i] * cot_plane(i)
        store_plane(back, i, v, count)
        keep_plane(weights, TOTAL - 1, i, v, count)

    for step in range(FINE_STEPS):
        up, down = step * SWEEPS, (FINE_STEPS - 1 - step) * SWEEPS
        final = down == 0
        for i in range(nx):
            sums[0, i] = scale[0, i] * even[i, body]

        def pair(n, c):
            k, m = up + 2 * n, down + SWEEPS - 1 - 2 * n
            two_sweeps(sz, coef, count, sums, (even, odd, fields, k + 1), (back, forth, weights, m - 1))
            two_sweeps(sz, coef, count, sums, (odd, even, fields, k + 2), (forth, back, weights, m - 2))
            return c

        lax.fori_loop(0, SWEEPS // 2 - final, pair, 0)
        if final:
            k = up + SWEEPS
            two_sweeps(sz, coef, count, sums, (even, odd, fields, k - 1), (back, forth, weights, 0))
            two_sweeps(sz, coef, count, sums, (odd, even, fields, k), None)
        else:
            for i in range(nx):
                total = weights[down, i, 0:count]
                for k in range(down + 1, down + SWEEPS):
                    total = total + weights[k, i, 0:count]
                v = back[i, body] + scale[0, i] * total
                store_plane(back, i, v, count)
                keep_plane(weights, down - 1, i, v, count)

    for i in range(nx):
        end_out[i] = even[i, body]
        for m, rough in enumerate(pack_rough(sz, lambda t: even[i, 1 + t])):
            rough_out[i, m] = rough

    def gather_sums(i, c):
        for t in range(count):
            along = [None, None, None]
            whole = None
            following = fields[0, i, t]
            for k in range(TOTAL):
                w, u, following = weights[k, i, t], following, fields[k + 1, i, t]
                for d, (up_w, up_u) in enumerate(
                    (
                        (weights[k, i + 1, t], fields[k, i + 1, t]),
                        (weights[k, i, t + 1], fields[k, i, t + 1]),
                        (z_up(w), z_up(u)),
                    )
                ):
                    term = w * up_u + up_w * u
                    along[d] = term if along[d] is None else along[d] + term
                term = w * following
                whole = term if whole is None else whole + term
            for d in range(3):
                sums[d, i, t] = along[d]
            even[i, t] = whole
            if t == 0:
                even[i, count] = next_sublane(whole)
        return c

    lax.fori_loop(0, nx, gather_sums, 0)
    rows = weights.reshape(TOTAL, nx + 1, (count + 1) * SUB, LANES)

    for i in range(nx):
        for t in range(count):
            here = even[i, t]
            for d, there in enumerate((even[i + 1, t] if i + 1 < nx else None, even[i, t + 1], z_up(here))):
                value = sums[d, i, t] - here
                if there is not None:
                    value = value - there
                rows[d, i, pl.ds(t, SUB, stride=count), :] = TIME_STEP * value

    for at in range(sz.spans):
        first = (turn ^ turned(at, sz.spans)) * sz.quarter
        for i in range(nx):
            dest, p = divmod(i, sz.planes)
            for g in range(sz.grad_tiles):
                tile = None
                for q in range(sz.factor):
                    n = g * sz.factor + q
                    if n >= sz.grad_parts:
                        continue
                    f, r = divmod(n, sz.share)
                    place = pl.ds(pl.multiple_of(first + r * SUB, SUB), SUB)
                    part = roll_lanes(rows[f, i, place, :], sz.own * q - sz.halo)
                    tile = part if tile is None else jnp.where(lane < sz.own * q, tile, part)
                row = (p * sz.grad_tiles + g) * SUB
                grads_out[at, dest, row : row + SUB, :] = tile


def rough_kernel(sz, start_ref, out_ref):
    for i in range(sz.nx):
        s, p = divmod(i, sz.planes)
        tile_of = lambda t: start_ref[s, (p * sz.tiles + t) * SUB : (p * sz.tiles + t + 1) * SUB, :]
        for m, rough in enumerate(pack_rough(sz, tile_of)):
            out_ref[i, m] = rough


def coarse_kernel(sz, *refs):
    pieces = refs[: sz.spans]
    jumps_ref, end_ref, out_ref = refs[sz.spans : sz.spans + 3]
    faces, rough, coef, scale, even, odd, source = refs[sz.spans + 3 :]
    nx, count = sz.nx, sz.tiles // 2
    body = slice(1, count + 1)
    turn = lax.axis_index("tm")
    lay_out_faces(sz, pieces, faces)
    for i in range(nx):
        for f, part in enumerate((1.0, 0.25, 0.25, 1.0)):
            for m in range(count):
                v = coarse_rows(lambda t: faces[f, i, t], m)
                rough[f, i, m] = v if part == 1.0 else part * v
    normalise(sz, rough, coef, scale, count, COARSE_STEP, 2)

    lane = lane_of((SUB, LANES))
    mine = (lane >= sz.halo) & (lane < sz.halo + sz.own)
    square = jnp.zeros((SUB, LANES), jnp.float32)
    for k in range(sz.spans - 1):
        for i in range(nx):
            for m in range(count // 2):
                square = square + jumps_ref[k, i, m] * jumps_ref[k, i, m]
    square = jnp.where(mine, square, 0.0)

    for d in reversed(range(1, sz.spans)):
        which = jnp.maximum(turn - d, 0)
        there = turn >= d
        for i in range(nx):
            jump = []
            for m in range(count // 2):
                jump += unpacked(jnp.where(there, jumps_ref[which, i, m], 0.0))
            v = jnp.stack(jump)
            if d < sz.spans - 1:
                v = v + even[i, body]
            store_plane(even, i, v, count)
            source[i] = scale[0, i] * v
        for n in range(COARSE_SWEEPS // 2):
            sweep(sz, coef, even, odd, count, 2, source)
            sweep(sz, coef, odd, even, count, 2, source)

    for i in range(nx):
        dest, p = divmod(i, sz.planes)
        for g in range(sz.end_tiles):
            tile = None
            for q in range(sz.factor):
                n = g * sz.factor + q
                part = roll_lanes(end_ref[i, n] + even[i, 1 + n // 2], sz.own * q - sz.halo)
                tile = part if tile is None else jnp.where(lane < sz.own * q, tile, part)
            row = (p * sz.end_tiles + g) * SUB
            out_ref[dest, row : row + SUB, :] = tile
    for s in range(sz.space):
        out_ref[s, sz.end_rows : sz.end_rows + SUB, :] = square


def join_kernel(sz, kept_ref, come_ref, ends_ref, out_ref):
    for s in range(sz.space):
        out_ref[s, : sz.grad_rows, :] = kept_ref[0, s] + come_ref[0, s]
        out_ref[s, sz.grad_rows :, :] = ends_ref[s]


def unpack_kernel(sz, in_ref, ends_out, gx_out, gy_out, gz_out, norm_out, rows):
    lane = lane_of((SUB, LANES))

    def whole_tile(tile, row, slot):
        result = None
        for q in range(sz.factor):
            block = tile * sz.factor + q
            part = roll_lanes(in_ref[block, row : row + SUB, :], sz.own * (q - slot))
            result = part if result is None else jnp.where(lane < sz.own * q, result, part)
        return result

    for t in range(sz.nz // LANES):
        columns = slice(t * LANES, (t + 1) * LANES)
        for p in range(sz.planes):
            for n in range(sz.grad_parts):
                f, r = divmod(n, sz.share)
                row = (p * sz.grad_tiles + n // sz.factor) * SUB
                (gx_out, gy_out, gz_out)[f][p, r * SUB : (r + 1) * SUB, columns] = whole_tile(t, row, n % sz.factor)
            for n in range(sz.end_parts):
                row = sz.grad_rows + (p * sz.end_tiles + n // sz.factor) * SUB
                rows[t, p, pl.ds(n, SUB, stride=sz.tiles), :] = whole_tile(t, row, n % sz.factor)
            ends_out[0, p, :, columns] = rows[t, p]
    squares = in_ref[0, sz.grad_rows + sz.end_rows :, :]
    for s in range(1, sz.space):
        squares = squares + in_ref[s, sz.grad_rows + sz.end_rows :, :]
    cells = (sz.spans - 1) * sz.nx * (sz.ny // 2) * (sz.nz // 2)
    whole = jnp.sum(jnp.sum(squares, axis=1, keepdims=True), axis=0, keepdims=True)
    norm_out[...] = jnp.sqrt(whole / cells)


def f32(*shape):
    return jax.ShapeDtypeStruct(shape, jnp.float32)


def call(kernel, sz, outs, scratch, *args, name, cost=None):
    held = sum(4 * math.prod(shape) for shape in scratch)
    held += sum(4 * math.prod(array.shape) for array in jax.tree.leaves((outs, args)))
    return pl.pallas_call(
        functools.partial(kernel, sz),
        out_shape=outs,
        scratch_shapes=[pltpu.VMEM(shape, jnp.float32) for shape in scratch],
        compiler_params=pltpu.CompilerParams(vmem_limit_bytes=held + SPARE_BYTES),
        cost_estimate=cost,
        name=name,
    )(*args)


def windows(kernel, sz, out, columns, *args, name):
    return pl.pallas_call(
        functools.partial(kernel, sz),
        out_shape=out,
        in_specs=[pl.BlockSpec(memory_space=pltpu.HBM)] * len(args),
        scratch_shapes=[pltpu.VMEM(array.shape, array.dtype) for array in args]
        + [pltpu.VMEM(columns, jnp.float32), pltpu.SemaphoreType.DMA((len(args),))],
        compiler_params=pltpu.CompilerParams(vmem_limit_bytes=60 * 1024 * 1024),
        name=name,
    )(*args)


def turned(index, size):
    result = 0
    while size > 1:
        result, index, size = result * 2 + index % 2, index // 2, size // 2
    return result


def exchange(values, axis, bit):
    size = lax.axis_size(axis)
    return lax.ppermute(values, axis, [(i, i ^ bit) for i in range(size)])


def shards(start_states, diff_x, diff_y, diff_z, stress, trap_class, cotangent):
    spans, space = lax.axis_size("tm"), lax.axis_size("space")
    sz = Sizes(spans, space, *diff_x.shape)
    nx, ny = sz.nx, sz.ny
    columns = (sz.planes, sz.nz // LANES, ny, LANES)
    coef = windows(
        face_windows_kernel,
        sz,
        f32(space, 4 * sz.planes * sz.quarter, LANES),
        (4,) + columns,
        diff_x,
        diff_y,
        diff_z,
        stress,
        trap_class,
        name="face_windows",
    )
    both = windows(
        field_windows_kernel,
        sz,
        f32(space, (sz.start_tiles + sz.cot_tiles) * SUB, LANES),
        (2,) + columns,
        start_states,
        cotangent,
        name="field_windows",
    )
    coef = lax.all_to_all(coef, "space", 0, 0)
    both = lax.all_to_all(both, "space", 0, 0)

    pieces = {0: coef}
    bit = spans // 2
    while bit:
        for key, piece in list(pieces.items()):
            pieces[key | bit] = exchange(piece, "tm", bit)
        bit //= 2
    pieces = [pieces[key] for key in range(spans)]

    tiles = sz.tiles
    rough_shape = f32(nx, tiles // 4, SUB, LANES)
    rough = call(rough_kernel, sz, rough_shape, (), both, name="rough")
    following = lax.ppermute(rough, "tm", [(i + 1, i) for i in range(spans - 1)])

    def field(count, *front):
        return front + (count, SUB, LANES)

    both, rough = lax.optimization_barrier((both, rough))
    coefs, scales = call(
        factors_kernel,
        sz,
        (f32(*field(tiles, 6, nx)), f32(*field(tiles, 2, nx))),
        (field(tiles, 4, nx),),
        *pieces,
        name="factors",
        cost=pl.CostEstimate(flops=40 * nx * ny * LANES, bytes_accessed=12 * 4 * nx * ny * LANES, transcendentals=0),
    )
    end, rough_end, grads = call(
        fine_kernel,
        sz,
        (f32(*field(tiles, nx)), rough_shape, f32(spans, space, sz.grad_rows, LANES)),
        (
            field(tiles, 3, nx),
            field(tiles + 2, nx),
            field(tiles + 2, nx),
            field(tiles + 2, nx),
            field(tiles + 2, nx),
            field(tiles + 1, TOTAL + 1, nx + 1),
            field(tiles + 1, TOTAL, nx + 1),
        ),
        coefs,
        scales,
        both,
        name="fine",
    )
    jumps = jnp.where(lax.axis_index("tm") == spans - 1, 0.0, rough_end - following)
    jumps = lax.all_gather(jumps, "tm", axis=0)

    half, bit = spans // 2, 1
    while half:
        come = exchange(grads[half:], "tm", bit)
        kept = grads[:half]
        if bit == 1:
            come, jumps = lax.optimization_barrier((come, jumps))
        grads = kept + come if half > 1 else None
        half, bit = half // 2, bit * 2

    ends = call(
        coarse_kernel,
        sz,
        f32(space, sz.end_rows + SUB, LANES),
        (
            field(tiles, 4, nx),
            field(tiles // 2, 4, nx),
            field(tiles // 2, 6, nx),
            field(tiles // 2, 2, nx),
            field(tiles // 2 + 2, nx),
            field(tiles // 2 + 2, nx),
            field(tiles // 2, nx),
        ),
        *pieces,
        jumps,
        end,
        name="coarse",
    )
    joined = call(join_kernel, sz, f32(space, sz.out_rows, LANES), (), kept, come, ends, name="join")
    joined = lax.all_to_all(joined, "space", 0, 0)
    quarter = f32(sz.planes, sz.quarter, sz.nz)
    new_end, gx, gy, gz, norm = call(
        unpack_kernel,
        sz,
        (f32(1, sz.planes, ny, sz.nz), quarter, quarter, quarter, f32(1, 1)),
        ((sz.nz // LANES, sz.planes, ny, LANES),),
        joined,
        name="unpack",
    )
    return new_end, gx, gy, gz, norm.reshape(())


def solution(mesh):
    fields = P("tm", "space", None, None)
    faces = P("space", None, None)
    quarter = P("space", "tm", None)
    return jax.shard_map(
        shards,
        mesh=mesh,
        in_specs=(fields, faces, faces, faces, faces, faces, fields),
        out_specs=(fields, quarter, quarter, quarter, P()),
        check_vma=False,
    )
```

```python
import functools
import math

import jax
import jax.numpy as jnp
from jax import lax
from jax.experimental import pallas as pl
from jax.experimental.pallas import tpu as pltpu
from jax.sharding import PartitionSpec as P

FINE_STEPS = 2
SWEEPS = 8
COARSE_SWEEPS = 2
TOTAL = FINE_STEPS * SWEEPS
LANES = 128
SUB = 8

STRESS_COUPLING = 0.5
TIME_STEP = 1.0
COARSE_STEP = FINE_STEPS * TIME_STEP
TRAP_LEVELS = (0.0, 1.0, 3.0, 7.0)

SPARE_BYTES = 3 * 512 * 1024


class Sizes:
    def __init__(self, spans, space, planes, ny, nz):
        self.spans = spans
        self.space = space
        self.planes = planes
        self.nx = planes * space
        self.ny = ny
        self.nz = nz
        self.own = nz // space
        self.halo = (LANES - self.own) // 2
        self.quarter = ny // spans
        self.share = self.quarter // SUB
        self.tiles = ny // SUB
        self.factor = LANES // self.own
        self.grad_parts = 3 * self.share
        self.grad_tiles = -(-self.grad_parts // self.factor)
        self.end_parts = self.tiles
        self.end_tiles = self.end_parts // self.factor
        self.grad_rows = planes * self.grad_tiles * SUB
        self.end_rows = planes * self.end_tiles * SUB
        self.out_rows = self.grad_rows + self.end_rows + SUB
        self.reach = TOTAL
        self.width = self.own + 2 * self.reach
        self.spare = LANES - self.width
        self.mains = self.width // self.spare
        self.start_tiles = planes * self.tiles
        self.cot_tiles = planes * self.tiles * self.mains // (self.mains + 1)
        assert self.mains * self.spare == self.width and self.start_tiles % (self.mains + 1) == 0
        assert self.tiles == SUB
        assert TOTAL + 2 * COARSE_SWEEPS * (spans - 1) <= self.halo


def lane_of(shape):
    return lax.broadcasted_iota(jnp.int32, shape, len(shape) - 1)


def row_of(shape):
    return lax.broadcasted_iota(jnp.int32, shape, len(shape) - 2)


def z_up(v, by=1):
    return pltpu.roll(v, LANES - by, v.ndim - 1)


def z_down(v, by=1):
    return pltpu.roll(v, by, v.ndim - 1)


def roll_lanes(v, by):
    by = by % LANES
    return v if by == 0 else pltpu.roll(v, by, 1)


def window(parts, first):
    lane = lane_of((SUB, LANES))
    zero = jnp.zeros((SUB, LANES), jnp.float32)
    tile, shift = first // LANES, first % LANES
    low = parts[tile] if 0 <= tile < len(parts) else zero
    if shift:
        high = parts[tile + 1] if tile + 1 < len(parts) else zero
        low = roll_lanes(jnp.where(lane < shift, high, low), -shift)
    return low


def start_copies(refs, count):
    copies = [pltpu.make_async_copy(refs[n], refs[count + 1 + n], refs[-1].at[n]) for n in range(count)]
    for copy in copies:
        copy.start()
    return copies


def face_windows_kernel(sz, *refs):
    fx_ref, fy_ref, fz_ref, stress_ref, trap_ref = refs[6:11]
    coef_out, columns = refs[5], refs[11]
    turn = lax.axis_index("tm")
    count = sz.nz // LANES
    copies = start_copies(refs, 5)

    def cut_field(f, p):
        for a in range(sz.share):
            rows = pl.ds(turn * sz.share + a, SUB, stride=sz.tiles)
            row = ((f * sz.planes + p) * sz.share + a) * SUB
            parts = [columns[f, p, n, rows, :] for n in range(count)]
            for j in range(sz.space):
                coef_out[j, row : row + SUB, :] = window(parts, sz.own * j - sz.halo)

    for f, ref in enumerate((fx_ref, fy_ref, fz_ref)):
        copies[f].wait()
        for p in range(sz.planes):
            for n in range(count):
                columns[f, p, n] = ref[p, :, n * LANES : (n + 1) * LANES]
            cut_field(f, p)
    copies[3].wait()
    copies[4].wait()
    for p in range(sz.planes):
        for n in range(count):
            cells = slice(n * LANES, (n + 1) * LANES)
            trap = trap_ref[p, :, cells]
            level = jnp.zeros(trap.shape, jnp.float32)
            for position, value in enumerate(TRAP_LEVELS):
                level = level + jnp.where(trap == position, value, 0.0)
            columns[3, p, n] = (1.0 + level) * jnp.exp(STRESS_COUPLING * stress_ref[p, :, cells])
        cut_field(3, p)


def field_windows_kernel(sz, *refs):
    start_ref, cot_ref = refs[3:5]
    field_out, ordered = refs[2], refs[5]
    count = sz.nz // LANES
    lane = lane_of((SUB, LANES))
    copies = start_copies(refs, 2)

    def tiled(ref, at):
        for p in range(sz.planes):
            for n in range(count):
                for r in range(SUB):
                    rows = slice(r * sz.tiles, (r + 1) * sz.tiles)
                    ordered[at, p, n, pl.ds(r, sz.tiles, stride=SUB), :] = ref[0, p, rows, n * LANES : (n + 1) * LANES]

    def tile_parts(at, q):
        p, t = divmod(q, sz.tiles)
        return [ordered[at, p, n, t * SUB : (t + 1) * SUB, :] for n in range(count)]

    copies[0].wait()
    tiled(start_ref, 0)
    for q in range(sz.start_tiles):
        parts = tile_parts(0, q)
        for j in range(sz.space):
            field_out[j, q * SUB : (q + 1) * SUB, :] = window(parts, sz.own * j - sz.halo)
    copies[1].wait()
    tiled(cot_ref, 1)
    for g in range(sz.cot_tiles // sz.mains):
        parts = [tile_parts(1, g * (sz.mains + 1) + q) for q in range(sz.mains + 1)]
        for j in range(sz.space):
            first = sz.own * j - sz.reach
            last = window(parts[sz.mains], first)
            for q in range(sz.mains):
                piece = roll_lanes(last, sz.width - sz.spare * q)
                row = (sz.start_tiles + g * sz.mains + q) * SUB
                field_out[j, row : row + SUB, :] = jnp.where(lane < sz.width, window(parts[q], first), piece)


def valid_columns(sz):
    column = lax.axis_index("space") * sz.own - sz.halo + lane_of((SUB, LANES))
    return (column >= 0) & (column < sz.nz)


def lay_out_faces(sz, pieces, faces):
    turn = lax.axis_index("tm")
    for key, piece in enumerate(pieces):
        for f in range(4):
            for p in range(sz.planes):
                for a in range(sz.share):
                    row = ((f * sz.planes + p) * sz.share + a) * SUB
                    for s in range(sz.space):
                        faces[f, s * sz.planes + p, (turn ^ key) * sz.share + a] = piece[s, row : row + SUB, :]


def next_sublane(v):
    return jnp.where(row_of(v.shape) == SUB - 1, 0.0, pltpu.roll(v, SUB - 1, v.ndim - 2))


def last_sublane(v):
    return jnp.where(row_of(v.shape) == 0, 0.0, pltpu.roll(v, 1, v.ndim - 2))


def normalise(sz, faces, coef, scale, count, step, apart):
    valid = valid_columns(sz)

    def one(i):
        for t in range(count):
            fx, fy, fz, cap = (faces[f, i, t] for f in range(4))
            bx = jnp.where(i == 0, 0.0, faces[0, jnp.maximum(i - 1, 0), t])
            by = faces[1, i, t - 1] if t else last_sublane(faces[1, i, count - 1])
            bz = z_down(fz, apart)
            diagonal = cap + step * (fx + bx + fy + by + fz + bz)
            inv = jnp.where(valid, 1.0 / diagonal, 0.0)
            scaled = step * inv
            for n, face in enumerate((fx, bx, fy, by, fz, bz)):
                coef[n, i, t] = face * scaled
            scale[0, i, t] = cap * inv
            scale[1, i, t] = inv

    def some(g, c):
        for q in range(4):
            one(4 * g + q)
        return c

    lax.fori_loop(0, sz.nx // 4, some, 0)


def store_plane(ref, at, v, count):
    ref[at, 0] = last_sublane(v[count - 1])
    ref[at, 1 : count + 1] = v
    ref[at, count + 1] = next_sublane(v[0])


def sweep(sz, coef, now, later, count, apart, source=None, kept=None):
    for i in range(sz.nx):
        v = now[i, 1 : count + 1]
        result = coef[2, i] * now[i, 2 : count + 2] + coef[3, i] * now[i, 0:count]
        result = result + coef[4, i] * z_up(v, apart) + coef[5, i] * z_down(v, apart)
        if i + 1 < sz.nx:
            result = result + coef[0, i] * now[i + 1, 1 : count + 1]
        if i:
            result = result + coef[1, i] * now[i - 1, 1 : count + 1]
        if source is not None:
            result = result + source[i]
        store_plane(later, i, result, count)
        if kept is not None:
            keep_plane(kept[0], kept[1], i, result, count)


def two_sweeps(sz, coef, count, source, forward, adjoint):
    for i in range(sz.nx):
        factors = [coef[n, i] for n in range(6)]
        for job in (forward, adjoint):
            if job is None:
                continue
            now, later, kept, at = job
            v = now[i, 1 : count + 1]
            result = factors[2] * now[i, 2 : count + 2] + factors[3] * now[i, 0:count]
            result = result + factors[4] * z_up(v) + factors[5] * z_down(v)
            if i + 1 < sz.nx:
                result = result + factors[0] * now[i + 1, 1 : count + 1]
            if i:
                result = result + factors[1] * now[i - 1, 1 : count + 1]
            if job is forward:
                result = result + source[0, i]
            store_plane(later, i, result, count)
            if kept is not None:
                keep_plane(kept, at, i, result, count)


def keep_plane(ref, k, i, v, count):
    ref[k, i, 0:count] = v
    ref[k, i, count] = next_sublane(v[0])


def coarse_rows(tile_of, m):
    v = tile_of(2 * m) + tile_of(2 * m + 1)
    return 0.25 * (v + jnp.where(lane_of(v.shape) % 2 == 0, z_up(v), z_down(v)))


def packed(low, high):
    return jnp.where(lane_of(low.shape) % 2 == 0, low, high)


def unpacked(v):
    even = lane_of(v.shape) % 2 == 0
    return jnp.where(even, v, z_down(v)), jnp.where(even, z_up(v), v)


def pack_rough(sz, tile_of):
    return [packed(coarse_rows(tile_of, 2 * m), coarse_rows(tile_of, 2 * m + 1)) for m in range(sz.tiles // 4)]


def factors_kernel(sz, *refs):
    pieces = refs[: sz.spans]
    coef_out, scale_out, faces = refs[sz.spans :]
    lay_out_faces(sz, pieces, faces)
    normalise(sz, faces, coef_out, scale_out, sz.tiles, TIME_STEP, 1)


def fine_kernel(sz, *refs):
    coef, scale, field_ref, following_ref, end_out, jump_out, grads_out = refs[:7]
    sums, even, odd, back, forth, fields, weights = refs[7:]
    nx, count = sz.nx, sz.tiles
    body = slice(1, count + 1)
    turn = lax.axis_index("tm")

    rim = jnp.zeros((count + 1, SUB, LANES), jnp.float32)
    for k in range(TOTAL + 1):
        fields[k, nx] = rim
        if k:
            weights[k - 1, nx] = rim

    lane = lane_of((SUB, LANES))
    aside = sz.halo - sz.reach

    def start_plane(i):
        s, p = divmod(i, sz.planes)
        return field_ref[s, p * sz.ny : (p + 1) * sz.ny, :].reshape(count, SUB, LANES)

    def cot_tile(s, n):
        g, q = divmod(n, sz.mains + 1)
        mains = [sz.start_tiles + g * sz.mains + m for m in range(sz.mains)]
        main = lambda m: field_ref[s, mains[m] * SUB : (mains[m] + 1) * SUB, :]
        if q < sz.mains:
            return roll_lanes(main(q), aside)
        result = None
        for m in range(sz.mains):
            part = roll_lanes(main(m), sz.spare * m - sz.width + aside)
            result = part if result is None else jnp.where(lane < sz.spare * m + aside, result, part)
        return result

    def cot_plane(i):
        s, p = divmod(i, sz.planes)
        return jnp.stack([cot_tile(s, p * count + t) for t in range(count)])

    for i in range(nx):
        v = start_plane(i)
        store_plane(even, i, v, count)
        keep_plane(fields, 0, i, v, count)
        v = scale[1, i] * cot_plane(i)
        store_plane(back, i, v, count)
        keep_plane(weights, TOTAL - 1, i, v, count)

    for step in range(FINE_STEPS):
        up, down = step * SWEEPS, (FINE_STEPS - 1 - step) * SWEEPS
        final = down == 0
        for i in range(nx):
            sums[0, i] = scale[0, i] * even[i, body]

        def pair(n, c):
            k, m = up + 2 * n, down + SWEEPS - 1 - 2 * n
            two_sweeps(sz, coef, count, sums, (even, odd, fields, k + 1), (back, forth, weights, m - 1))
            two_sweeps(sz, coef, count, sums, (odd, even, fields, k + 2), (forth, back, weights, m - 2))
            return c

        lax.fori_loop(0, SWEEPS // 2 - final, pair, 0)
        if final:
            k = up + SWEEPS
            two_sweeps(sz, coef, count, sums, (even, odd, fields, k - 1), (back, forth, weights, 0))
            two_sweeps(sz, coef, count, sums, (odd, even, fields, k), None)
        else:
            for i in range(nx):
                total = weights[down, i, 0:count]
                for k in range(down + 1, down + SWEEPS):
                    total = total + weights[k, i, 0:count]
                v = back[i, body] + scale[0, i] * total
                store_plane(back, i, v, count)
                keep_plane(weights, down - 1, i, v, count)

    last = turn == sz.spans - 1
    for i in range(nx):
        end_out[i] = even[i, body]
        for m, rough in enumerate(pack_rough(sz, lambda t: even[i, 1 + t])):
            jump_out[i, m] = jnp.where(last, 0.0, rough - following_ref[i, m])

    def gather_sums(i, c):
        for t in range(count):
            along = [None, None, None]
            whole = None
            following = fields[0, i, t]
            for k in range(TOTAL):
                w, u, following = weights[k, i, t], following, fields[k + 1, i, t]
                for d, (up_w, up_u) in enumerate(
                    (
                        (weights[k, i + 1, t], fields[k, i + 1, t]),
                        (weights[k, i, t + 1], fields[k, i, t + 1]),
                        (z_up(w), z_up(u)),
                    )
                ):
                    term = w * up_u + up_w * u
                    along[d] = term if along[d] is None else along[d] + term
                term = w * following
                whole = term if whole is None else whole + term
            for d in range(3):
                sums[d, i, t] = along[d]
            even[i, t] = whole
            if t == 0:
                even[i, count] = next_sublane(whole)
        return c

    lax.fori_loop(0, nx, gather_sums, 0)
    rows = weights.reshape(TOTAL, nx + 1, (count + 1) * SUB, LANES)

    for i in range(nx):
        for t in range(count):
            here = even[i, t]
            for d, there in enumerate((even[i + 1, t] if i + 1 < nx else None, even[i, t + 1], z_up(here))):
                value = sums[d, i, t] - here
                if there is not None:
                    value = value - there
                rows[d, i, pl.ds(t, SUB, stride=count), :] = TIME_STEP * value

    for at in range(sz.spans):
        first = (turn ^ turned(at, sz.spans)) * sz.quarter
        for i in range(nx):
            dest, p = divmod(i, sz.planes)
            for g in range(sz.grad_tiles):
                tile = None
                for q in range(sz.factor):
                    n = g * sz.factor + q
                    if n >= sz.grad_parts:
                        continue
                    f, r = divmod(n, sz.share)
                    place = pl.ds(pl.multiple_of(first + r * SUB, SUB), SUB)
                    part = roll_lanes(rows[f, i, place, :], sz.own * q - sz.halo)
                    tile = part if tile is None else jnp.where(lane < sz.own * q, tile, part)
                row = (p * sz.grad_tiles + g) * SUB
                grads_out[at, dest, row : row + SUB, :] = tile


def rough_kernel(sz, start_ref, out_ref):
    for i in range(sz.nx):
        s, p = divmod(i, sz.planes)
        tile_of = lambda t: start_ref[s, (p * sz.tiles + t) * SUB : (p * sz.tiles + t + 1) * SUB, :]
        for m, rough in enumerate(pack_rough(sz, tile_of)):
            out_ref[i, m] = rough


def coarse_kernel(sz, *refs):
    pieces = refs[: sz.spans]
    parts = refs[sz.spans : 2 * sz.spans]
    end_ref, out_ref, faces, rough, coef, scale, even, odd, source, jumps = refs[2 * sz.spans :]
    nx, count = sz.nx, sz.tiles // 2
    body = slice(1, count + 1)
    turn = lax.axis_index("tm")
    lay_out_faces(sz, pieces, faces)
    for i in range(nx):
        for f, part in enumerate((1.0, 0.25, 0.25, 1.0)):
            for m in range(count):
                v = coarse_rows(lambda t: faces[f, i, t], m)
                rough[f, i, m] = v if part == 1.0 else part * v
    normalise(sz, rough, coef, scale, count, COARSE_STEP, 2)

    lane = lane_of((SUB, LANES))
    mine = (lane >= sz.halo) & (lane < sz.halo + sz.own)
    square = jnp.zeros((SUB, LANES), jnp.float32)
    for key, part in enumerate(parts):
        for i in range(nx):
            for m in range(count // 2):
                jump = part[i, m]
                jumps[key, i, m] = jump
                square = square + jump * jump
    square = jnp.where(mine, square, 0.0)

    for d in reversed(range(1, sz.spans)):
        which = jnp.maximum(turn - d, 0)
        there = turn >= d
        for i in range(nx):
            jump = []
            for m in range(count // 2):
                jump += unpacked(jnp.where(there, jumps[turn ^ which, i, m], 0.0))
            v = jnp.stack(jump)
            if d < sz.spans - 1:
                v = v + even[i, body]
            store_plane(even, i, v, count)
            source[i] = scale[0, i] * v
        for n in range(COARSE_SWEEPS // 2):
            sweep(sz, coef, even, odd, count, 2, source)
            sweep(sz, coef, odd, even, count, 2, source)

    for i in range(nx):
        dest, p = divmod(i, sz.planes)
        for g in range(sz.end_tiles):
            tile = None
            for q in range(sz.factor):
                n = g * sz.factor + q
                part = roll_lanes(end_ref[i, n] + even[i, 1 + n // 2], sz.own * q - sz.halo)
                tile = part if tile is None else jnp.where(lane < sz.own * q, tile, part)
            row = (p * sz.end_tiles + g) * SUB
            out_ref[dest, row : row + SUB, :] = tile
    for s in range(sz.space):
        out_ref[s, sz.end_rows : sz.end_rows + SUB, :] = square


def join_kernel(sz, kept_ref, come_ref, ends_ref, out_ref):
    for s in range(sz.space):
        out_ref[s, : sz.grad_rows, :] = kept_ref[0, s] + come_ref[0, s]
        out_ref[s, sz.grad_rows :, :] = ends_ref[s]


def unpack_kernel(sz, in_ref, ends_out, gx_out, gy_out, gz_out, norm_out, rows):
    lane = lane_of((SUB, LANES))

    def whole_tile(tile, row, slot):
        result = None
        for q in range(sz.factor):
            block = tile * sz.factor + q
            part = roll_lanes(in_ref[block, row : row + SUB, :], sz.own * (q - slot))
            result = part if result is None else jnp.where(lane < sz.own * q, result, part)
        return result

    for t in range(sz.nz // LANES):
        columns = slice(t * LANES, (t + 1) * LANES)
        for p in range(sz.planes):
            for n in range(sz.grad_parts):
                f, r = divmod(n, sz.share)
                row = (p * sz.grad_tiles + n // sz.factor) * SUB
                (gx_out, gy_out, gz_out)[f][p, r * SUB : (r + 1) * SUB, columns] = whole_tile(t, row, n % sz.factor)
            for n in range(sz.end_parts):
                row = sz.grad_rows + (p * sz.end_tiles + n // sz.factor) * SUB
                rows[t, p, pl.ds(n, SUB, stride=sz.tiles), :] = whole_tile(t, row, n % sz.factor)
            ends_out[0, p, :, columns] = rows[t, p]
    squares = in_ref[0, sz.grad_rows + sz.end_rows :, :]
    for s in range(1, sz.space):
        squares = squares + in_ref[s, sz.grad_rows + sz.end_rows :, :]
    cells = (sz.spans - 1) * sz.nx * (sz.ny // 2) * (sz.nz // 2)
    whole = jnp.sum(jnp.sum(squares, axis=1, keepdims=True), axis=0, keepdims=True)
    norm_out[...] = jnp.sqrt(whole / cells)


def f32(*shape):
    return jax.ShapeDtypeStruct(shape, jnp.float32)


def call(kernel, sz, outs, scratch, *args, name, cost=None):
    held = sum(4 * math.prod(shape) for shape in scratch)
    held += sum(4 * math.prod(array.shape) for array in jax.tree.leaves((outs, args)))
    return pl.pallas_call(
        functools.partial(kernel, sz),
        out_shape=outs,
        scratch_shapes=[pltpu.VMEM(shape, jnp.float32) for shape in scratch],
        compiler_params=pltpu.CompilerParams(vmem_limit_bytes=held + SPARE_BYTES),
        cost_estimate=cost,
        name=name,
    )(*args)


def windows(kernel, sz, out, columns, *args, name):
    return pl.pallas_call(
        functools.partial(kernel, sz),
        out_shape=out,
        in_specs=[pl.BlockSpec(memory_space=pltpu.HBM)] * len(args),
        scratch_shapes=[pltpu.VMEM(array.shape, array.dtype) for array in args]
        + [pltpu.VMEM(columns, jnp.float32), pltpu.SemaphoreType.DMA((len(args),))],
        compiler_params=pltpu.CompilerParams(vmem_limit_bytes=60 * 1024 * 1024),
        name=name,
    )(*args)


def turned(index, size):
    result = 0
    while size > 1:
        result, index, size = result * 2 + index % 2, index // 2, size // 2
    return result


def exchange(values, axis, bit):
    size = lax.axis_size(axis)
    return lax.ppermute(values, axis, [(i, i ^ bit) for i in range(size)])


def from_all(values, axis):
    pieces, bit = {0: values}, lax.axis_size(axis) // 2
    while bit:
        for key, piece in list(pieces.items()):
            pieces[key | bit] = exchange(piece, axis, bit)
        bit //= 2
    return [pieces[key] for key in range(len(pieces))]


def shards(start_states, diff_x, diff_y, diff_z, stress, trap_class, cotangent):
    spans, space = lax.axis_size("tm"), lax.axis_size("space")
    sz = Sizes(spans, space, *diff_x.shape)
    nx, ny = sz.nx, sz.ny
    columns = (sz.planes, sz.nz // LANES, ny, LANES)
    coef = windows(
        face_windows_kernel,
        sz,
        f32(space, 4 * sz.planes * sz.quarter, LANES),
        (4,) + columns,
        diff_x,
        diff_y,
        diff_z,
        stress,
        trap_class,
        name="face_windows",
    )
    both = windows(
        field_windows_kernel,
        sz,
        f32(space, (sz.start_tiles + sz.cot_tiles) * SUB, LANES),
        (2,) + columns,
        start_states,
        cotangent,
        name="field_windows",
    )
    coef = lax.all_to_all(coef, "space", 0, 0)
    both = lax.all_to_all(both, "space", 0, 0)

    pieces = from_all(coef, "tm")

    tiles = sz.tiles
    rough_shape = f32(nx, tiles // 4, SUB, LANES)
    rough = call(rough_kernel, sz, rough_shape, (), both, name="rough")
    following = lax.ppermute(rough, "tm", [(i + 1, i) for i in range(spans - 1)])

    def field(count, *front):
        return front + (count, SUB, LANES)

    coefs, scales = call(
        factors_kernel,
        sz,
        (f32(*field(tiles, 6, nx)), f32(*field(tiles, 2, nx))),
        (field(tiles, 4, nx),),
        *pieces,
        name="factors",
        cost=pl.CostEstimate(flops=40 * nx * ny * LANES, bytes_accessed=12 * 4 * nx * ny * LANES, transcendentals=0),
    )
    end, jumps, grads = call(
        fine_kernel,
        sz,
        (f32(*field(tiles, nx)), rough_shape, f32(spans, space, sz.grad_rows, LANES)),
        (
            field(tiles, 3, nx),
            field(tiles + 2, nx),
            field(tiles + 2, nx),
            field(tiles + 2, nx),
            field(tiles + 2, nx),
            field(tiles + 1, TOTAL + 1, nx + 1),
            field(tiles + 1, TOTAL, nx + 1),
        ),
        coefs,
        scales,
        both,
        following,
        name="fine",
    )
    jumps = from_all(jumps, "tm")

    half, bit = spans // 2, 1
    while half:
        come = exchange(grads[half:], "tm", bit)
        kept = grads[:half]
        grads = kept + come if half > 1 else None
        half, bit = half // 2, bit * 2

    ends = call(
        coarse_kernel,
        sz,
        f32(space, sz.end_rows + SUB, LANES),
        (
            field(tiles, 4, nx),
            field(tiles // 2, 4, nx),
            field(tiles // 2, 6, nx),
            field(tiles // 2, 2, nx),
            field(tiles // 2 + 2, nx),
            field(tiles // 2 + 2, nx),
            field(tiles // 2, nx),
            field(tiles // 4, spans, nx),
        ),
        *pieces,
        *jumps,
        end,
        name="coarse",
    )
    joined = call(join_kernel, sz, f32(space, sz.out_rows, LANES), (), kept, come, ends, name="join")
    joined = lax.all_to_all(joined, "space", 0, 0)
    quarter = f32(sz.planes, sz.quarter, sz.nz)
    new_end, gx, gy, gz, norm = call(
        unpack_kernel,
        sz,
        (f32(1, sz.planes, ny, sz.nz), quarter, quarter, quarter, f32(1, 1)),
        ((sz.nz // LANES, sz.planes, ny, LANES),),
        joined,
        name="unpack",
    )
    return new_end, gx, gy, gz, norm.reshape(())


def solution(mesh):
    fields = P("tm", "space", None, None)
    faces = P("space", None, None)
    quarter = P("space", "tm", None)
    return jax.shard_map(
        shards,
        mesh=mesh,
        in_specs=(fields, faces, faces, faces, faces, faces, fields),
        out_specs=(fields, quarter, quarter, quarter, P()),
        check_vma=False,
    )
```

```python
import functools
import math

import jax
import jax.numpy as jnp
from jax import lax
from jax.experimental import pallas as pl
from jax.experimental.pallas import tpu as pltpu
from jax.sharding import PartitionSpec as P

FINE_STEPS = 2
SWEEPS = 8
COARSE_SWEEPS = 2
TOTAL = FINE_STEPS * SWEEPS
LANES = 128
SUB = 8

STRESS_COUPLING = 0.5
TIME_STEP = 1.0
COARSE_STEP = FINE_STEPS * TIME_STEP
TRAP_LEVELS = (0.0, 1.0, 3.0, 7.0)

SPARE_BYTES = 3 * 512 * 1024


class Sizes:
    def __init__(self, spans, space, planes, ny, nz):
        self.spans = spans
        self.space = space
        self.planes = planes
        self.nx = planes * space
        self.ny = ny
        self.nz = nz
        self.own = nz // space
        self.halo = (LANES - self.own) // 2
        self.quarter = ny // spans
        self.share = self.quarter // SUB
        self.tiles = ny // SUB
        self.factor = LANES // self.own
        self.grad_parts = 3 * self.share
        self.grad_tiles = -(-self.grad_parts // self.factor)
        self.end_parts = self.tiles
        self.end_tiles = self.end_parts // self.factor
        self.grad_rows = planes * self.grad_tiles * SUB
        self.end_rows = planes * self.end_tiles * SUB
        self.out_rows = self.grad_rows + self.end_rows + SUB
        self.reach = TOTAL
        self.width = self.own + 2 * self.reach
        self.spare = LANES - self.width
        self.mains = self.width // self.spare
        self.start_tiles = planes * self.tiles
        self.cot_tiles = planes * self.tiles * self.mains // (self.mains + 1)
        assert self.mains * self.spare == self.width and self.start_tiles % (self.mains + 1) == 0
        assert self.tiles == SUB
        assert TOTAL + 2 * COARSE_SWEEPS * (spans - 1) <= self.halo


def lane_of(shape):
    return lax.broadcasted_iota(jnp.int32, shape, len(shape) - 1)


def row_of(shape):
    return lax.broadcasted_iota(jnp.int32, shape, len(shape) - 2)


def z_up(v, by=1):
    return pltpu.roll(v, LANES - by, v.ndim - 1)


def z_down(v, by=1):
    return pltpu.roll(v, by, v.ndim - 1)


def roll_lanes(v, by):
    by = by % LANES
    return v if by == 0 else pltpu.roll(v, by, 1)


def window(parts, first):
    lane = lane_of((SUB, LANES))
    zero = jnp.zeros((SUB, LANES), jnp.float32)
    tile, shift = first // LANES, first % LANES
    low = parts[tile] if 0 <= tile < len(parts) else zero
    if shift:
        high = parts[tile + 1] if tile + 1 < len(parts) else zero
        low = roll_lanes(jnp.where(lane < shift, high, low), -shift)
    return low


def start_copies(refs, count):
    copies = [pltpu.make_async_copy(refs[n], refs[count + 1 + n], refs[-1].at[n]) for n in range(count)]
    for copy in copies:
        copy.start()
    return copies


def face_windows_kernel(sz, *refs):
    fx_ref, fy_ref, fz_ref, stress_ref, trap_ref = refs[6:11]
    coef_out, columns = refs[5], refs[11]
    turn = lax.axis_index("tm")
    count = sz.nz // LANES
    copies = start_copies(refs, 5)

    def cut_field(f, p):
        for a in range(sz.share):
            rows = pl.ds(turn * sz.share + a, SUB, stride=sz.tiles)
            row = ((f * sz.planes + p) * sz.share + a) * SUB
            parts = [columns[f, p, n, rows, :] for n in range(count)]
            for j in range(sz.space):
                coef_out[j, row : row + SUB, :] = window(parts, sz.own * j - sz.halo)

    for f, ref in enumerate((fx_ref, fy_ref, fz_ref)):
        copies[f].wait()
        for p in range(sz.planes):
            for n in range(count):
                columns[f, p, n] = ref[p, :, n * LANES : (n + 1) * LANES]
            cut_field(f, p)
    copies[3].wait()
    copies[4].wait()
    for p in range(sz.planes):
        for n in range(count):
            cells = slice(n * LANES, (n + 1) * LANES)
            trap = trap_ref[p, :, cells]
            level = jnp.zeros(trap.shape, jnp.float32)
            for position, value in enumerate(TRAP_LEVELS):
                level = level + jnp.where(trap == position, value, 0.0)
            columns[3, p, n] = (1.0 + level) * jnp.exp(STRESS_COUPLING * stress_ref[p, :, cells])
        cut_field(3, p)


def field_windows_kernel(sz, *refs):
    start_ref, cot_ref = refs[3:5]
    field_out, ordered = refs[2], refs[5]
    count = sz.nz // LANES
    lane = lane_of((SUB, LANES))
    copies = start_copies(refs, 2)

    def tiled(ref, at):
        for p in range(sz.planes):
            for n in range(count):
                for r in range(SUB):
                    rows = slice(r * sz.tiles, (r + 1) * sz.tiles)
                    ordered[at, p, n, pl.ds(r, sz.tiles, stride=SUB), :] = ref[0, p, rows, n * LANES : (n + 1) * LANES]

    def tile_parts(at, q):
        p, t = divmod(q, sz.tiles)
        return [ordered[at, p, n, t * SUB : (t + 1) * SUB, :] for n in range(count)]

    copies[0].wait()
    tiled(start_ref, 0)
    for q in range(sz.start_tiles):
        parts = tile_parts(0, q)
        for j in range(sz.space):
            field_out[j, q * SUB : (q + 1) * SUB, :] = window(parts, sz.own * j - sz.halo)
    copies[1].wait()
    tiled(cot_ref, 1)
    for g in range(sz.cot_tiles // sz.mains):
        parts = [tile_parts(1, g * (sz.mains + 1) + q) for q in range(sz.mains + 1)]
        for j in range(sz.space):
            first = sz.own * j - sz.reach
            last = window(parts[sz.mains], first)
            for q in range(sz.mains):
                piece = roll_lanes(last, sz.width - sz.spare * q)
                row = (sz.start_tiles + g * sz.mains + q) * SUB
                field_out[j, row : row + SUB, :] = jnp.where(lane < sz.width, window(parts[q], first), piece)


def valid_columns(sz):
    column = lax.axis_index("space") * sz.own - sz.halo + lane_of((SUB, LANES))
    return (column >= 0) & (column < sz.nz)


def lay_out_faces(sz, pieces, faces):
    turn = lax.axis_index("tm")
    for key, piece in enumerate(pieces):
        for f in range(4):
            for p in range(sz.planes):
                for a in range(sz.share):
                    row = ((f * sz.planes + p) * sz.share + a) * SUB
                    for s in range(sz.space):
                        faces[f, s * sz.planes + p, (turn ^ key) * sz.share + a] = piece[s, row : row + SUB, :]


def next_sublane(v):
    return jnp.where(row_of(v.shape) == SUB - 1, 0.0, pltpu.roll(v, SUB - 1, v.ndim - 2))


def last_sublane(v):
    return jnp.where(row_of(v.shape) == 0, 0.0, pltpu.roll(v, 1, v.ndim - 2))


def normalise(sz, faces, coef, scale, count, step, apart):
    valid = valid_columns(sz)

    def one(i):
        for t in range(count):
            fx, fy, fz, cap = (faces[f, i, t] for f in range(4))
            bx = jnp.where(i == 0, 0.0, faces[0, jnp.maximum(i - 1, 0), t])
            by = faces[1, i, t - 1] if t else last_sublane(faces[1, i, count - 1])
            bz = z_down(fz, apart)
            diagonal = cap + step * (fx + bx + fy + by + fz + bz)
            inv = jnp.where(valid, 1.0 / diagonal, 0.0)
            scaled = step * inv
            for n, face in enumerate((fx, bx, fy, by, fz, bz)):
                coef[n, i, t] = face * scaled
            scale[0, i, t] = cap * inv
            scale[1, i, t] = inv

    def some(g, c):
        for q in range(4):
            one(4 * g + q)
        return c

    lax.fori_loop(0, sz.nx // 4, some, 0)


def store_plane(ref, at, v, count):
    ref[at, 0] = last_sublane(v[count - 1])
    ref[at, 1 : count + 1] = v
    ref[at, count + 1] = next_sublane(v[0])


def sweep(sz, coef, now, later, count, apart, source=None, kept=None):
    for i in range(sz.nx):
        v = now[i, 1 : count + 1]
        result = coef[2, i] * now[i, 2 : count + 2] + coef[3, i] * now[i, 0:count]
        result = result + coef[4, i] * z_up(v, apart) + coef[5, i] * z_down(v, apart)
        if i + 1 < sz.nx:
            result = result + coef[0, i] * now[i + 1, 1 : count + 1]
        if i:
            result = result + coef[1, i] * now[i - 1, 1 : count + 1]
        if source is not None:
            result = result + source[i]
        store_plane(later, i, result, count)
        if kept is not None:
            keep_plane(kept[0], kept[1], i, result, count)


def two_sweeps(sz, coef, count, source, forward, adjoint):
    for i in range(sz.nx):
        factors = [coef[n, i] for n in range(6)]
        for job in (forward, adjoint):
            if job is None:
                continue
            now, later, kept, at = job
            v = now[i, 1 : count + 1]
            result = factors[2] * now[i, 2 : count + 2] + factors[3] * now[i, 0:count]
            result = result + factors[4] * z_up(v) + factors[5] * z_down(v)
            if i + 1 < sz.nx:
                result = result + factors[0] * now[i + 1, 1 : count + 1]
            if i:
                result = result + factors[1] * now[i - 1, 1 : count + 1]
            if job is forward:
                result = result + source[0, i]
            store_plane(later, i, result, count)
            if kept is not None:
                keep_plane(kept, at, i, result, count)


def keep_plane(ref, k, i, v, count):
    ref[k, i, 0:count] = v
    ref[k, i, count] = next_sublane(v[0])


def coarse_rows(tile_of, m):
    v = tile_of(2 * m) + tile_of(2 * m + 1)
    return 0.25 * (v + jnp.where(lane_of(v.shape) % 2 == 0, z_up(v), z_down(v)))


def packed(low, high):
    return jnp.where(lane_of(low.shape) % 2 == 0, low, high)


def unpacked(v):
    even = lane_of(v.shape) % 2 == 0
    return jnp.where(even, v, z_down(v)), jnp.where(even, z_up(v), v)


def pack_rough(sz, tile_of):
    return [packed(coarse_rows(tile_of, 2 * m), coarse_rows(tile_of, 2 * m + 1)) for m in range(sz.tiles // 4)]


def factors_kernel(sz, *refs):
    pieces = refs[: sz.spans]
    coef_out, scale_out, faces = refs[sz.spans :]
    lay_out_faces(sz, pieces, faces)
    normalise(sz, faces, coef_out, scale_out, sz.tiles, TIME_STEP, 1)


def fine_kernel(sz, *refs):
    coef, scale, field_ref, following_ref, end_out, jump_out, grads_out = refs[:7]
    sums, even, odd, back, forth, fields, weights = refs[7:]
    nx, count = sz.nx, sz.tiles
    body = slice(1, count + 1)
    turn = lax.axis_index("tm")

    rim = jnp.zeros((count + 1, SUB, LANES), jnp.float32)
    for k in range(TOTAL + 1):
        fields[k, nx] = rim
        if k:
            weights[k - 1, nx] = rim

    lane = lane_of((SUB, LANES))
    aside = sz.halo - sz.reach

    def start_plane(i):
        s, p = divmod(i, sz.planes)
        return field_ref[s, p * sz.ny : (p + 1) * sz.ny, :].reshape(count, SUB, LANES)

    def cot_tile(s, n):
        g, q = divmod(n, sz.mains + 1)
        mains = [sz.start_tiles + g * sz.mains + m for m in range(sz.mains)]
        main = lambda m: field_ref[s, mains[m] * SUB : (mains[m] + 1) * SUB, :]
        if q < sz.mains:
            return roll_lanes(main(q), aside)
        result = None
        for m in range(sz.mains):
            part = roll_lanes(main(m), sz.spare * m - sz.width + aside)
            result = part if result is None else jnp.where(lane < sz.spare * m + aside, result, part)
        return result

    def cot_plane(i):
        s, p = divmod(i, sz.planes)
        return jnp.stack([cot_tile(s, p * count + t) for t in range(count)])

    for i in range(nx):
        v = start_plane(i)
        store_plane(even, i, v, count)
        keep_plane(fields, 0, i, v, count)
        v = scale[1, i] * cot_plane(i)
        store_plane(back, i, v, count)
        keep_plane(weights, TOTAL - 1, i, v, count)

    for step in range(FINE_STEPS):
        up, down = step * SWEEPS, (FINE_STEPS - 1 - step) * SWEEPS
        final = down == 0
        for i in range(nx):
            sums[0, i] = scale[0, i] * even[i, body]

        def pair(n, c):
            k, m = up + 2 * n, down + SWEEPS - 1 - 2 * n
            two_sweeps(sz, coef, count, sums, (even, odd, fields, k + 1), (back, forth, weights, m - 1))
            two_sweeps(sz, coef, count, sums, (odd, even, fields, k + 2), (forth, back, weights, m - 2))
            return c

        lax.fori_loop(0, SWEEPS // 2 - final, pair, 0)
        if final:
            k = up + SWEEPS
            two_sweeps(sz, coef, count, sums, (even, odd, fields, k - 1), (back, forth, weights, 0))
            two_sweeps(sz, coef, count, sums, (odd, even, fields, k), None)
        else:
            for i in range(nx):
                total = weights[down, i, 0:count]
                for k in range(down + 1, down + SWEEPS):
                    total = total + weights[k, i, 0:count]
                v = back[i, body] + scale[0, i] * total
                store_plane(back, i, v, count)
                keep_plane(weights, down - 1, i, v, count)

    last = turn == sz.spans - 1
    for i in range(nx):
        end_out[i] = even[i, body]
        for m, rough in enumerate(pack_rough(sz, lambda t: even[i, 1 + t])):
            jump_out[i, m] = jnp.where(last, 0.0, rough - following_ref[i, m])

    def gather_sums(i, c):
        for t in range(count):
            along = [None, None, None]
            whole = None
            following = fields[0, i, t]
            for k in range(TOTAL):
                w, u, following = weights[k, i, t], following, fields[k + 1, i, t]
                for d, (up_w, up_u) in enumerate(
                    (
                        (weights[k, i + 1, t], fields[k, i + 1, t]),
                        (weights[k, i, t + 1], fields[k, i, t + 1]),
                        (z_up(w), z_up(u)),
                    )
                ):
                    term = w * up_u + up_w * u
                    along[d] = term if along[d] is None else along[d] + term
                term = w * following
                whole = term if whole is None else whole + term
            for d in range(3):
                sums[d, i, t] = along[d]
            even[i, t] = whole
            if t == 0:
                even[i, count] = next_sublane(whole)
        return c

    lax.fori_loop(0, nx, gather_sums, 0)
    rows = weights.reshape(TOTAL, nx + 1, (count + 1) * SUB, LANES)

    for i in range(nx):
        for t in range(count):
            here = even[i, t]
            for d, there in enumerate((even[i + 1, t] if i + 1 < nx else None, even[i, t + 1], z_up(here))):
                value = sums[d, i, t] - here
                if there is not None:
                    value = value - there
                rows[d, i, pl.ds(t, SUB, stride=count), :] = TIME_STEP * value

    for at in range(sz.spans):
        first = (turn ^ turned(at, sz.spans)) * sz.quarter
        for i in range(nx):
            dest, p = divmod(i, sz.planes)
            for g in range(sz.grad_tiles):
                tile = None
                for q in range(sz.factor):
                    n = g * sz.factor + q
                    if n >= sz.grad_parts:
                        continue
                    f, r = divmod(n, sz.share)
                    place = pl.ds(pl.multiple_of(first + r * SUB, SUB), SUB)
                    part = roll_lanes(rows[f, i, place, :], sz.own * q - sz.halo)
                    tile = part if tile is None else jnp.where(lane < sz.own * q, tile, part)
                row = (p * sz.grad_tiles + g) * SUB
                grads_out[at, dest, row : row + SUB, :] = tile


def rough_kernel(sz, start_ref, out_ref):
    for i in range(sz.nx):
        s, p = divmod(i, sz.planes)
        tile_of = lambda t: start_ref[s, (p * sz.tiles + t) * SUB : (p * sz.tiles + t + 1) * SUB, :]
        for m, rough in enumerate(pack_rough(sz, tile_of)):
            out_ref[i, m] = rough


def coarse_factors_kernel(sz, *refs):
    pieces = refs[: sz.spans]
    coef, scale, faces, rough = refs[sz.spans :]
    nx, count = sz.nx, sz.tiles // 2
    lay_out_faces(sz, pieces, faces)
    for i in range(nx):
        for f, part in enumerate((1.0, 0.25, 0.25, 1.0)):
            for m in range(count):
                v = coarse_rows(lambda t: faces[f, i, t], m)
                rough[f, i, m] = v if part == 1.0 else part * v
    normalise(sz, rough, coef, scale, count, COARSE_STEP, 2)


def coarse_kernel(sz, *refs):
    coef, scale = refs[:2]
    parts = refs[2 : 2 + sz.spans]
    end_ref, out_ref, even, odd, source, jumps = refs[2 + sz.spans :]
    nx, count = sz.nx, sz.tiles // 2
    body = slice(1, count + 1)
    turn = lax.axis_index("tm")

    lane = lane_of((SUB, LANES))
    mine = (lane >= sz.halo) & (lane < sz.halo + sz.own)
    square = jnp.zeros((SUB, LANES), jnp.float32)
    for key, part in enumerate(parts):
        for i in range(nx):
            for m in range(count // 2):
                jump = part[i, m]
                jumps[key, i, m] = jump
                square = square + jump * jump
    square = jnp.where(mine, square, 0.0)

    for d in reversed(range(1, sz.spans)):
        which = jnp.maximum(turn - d, 0)
        there = turn >= d
        for i in range(nx):
            jump = []
            for m in range(count // 2):
                jump += unpacked(jnp.where(there, jumps[turn ^ which, i, m], 0.0))
            v = jnp.stack(jump)
            if d < sz.spans - 1:
                v = v + even[i, body]
            store_plane(even, i, v, count)
            source[i] = scale[0, i] * v
        for n in range(COARSE_SWEEPS // 2):
            sweep(sz, coef, even, odd, count, 2, source)
            sweep(sz, coef, odd, even, count, 2, source)

    for i in range(nx):
        dest, p = divmod(i, sz.planes)
        for g in range(sz.end_tiles):
            tile = None
            for q in range(sz.factor):
                n = g * sz.factor + q
                part = roll_lanes(end_ref[i, n] + even[i, 1 + n // 2], sz.own * q - sz.halo)
                tile = part if tile is None else jnp.where(lane < sz.own * q, tile, part)
            row = (p * sz.end_tiles + g) * SUB
            out_ref[dest, row : row + SUB, :] = tile
    for s in range(sz.space):
        out_ref[s, sz.end_rows : sz.end_rows + SUB, :] = square


def join_kernel(sz, kept_ref, come_ref, ends_ref, out_ref):
    for s in range(sz.space):
        out_ref[s, : sz.grad_rows, :] = kept_ref[0, s] + come_ref[0, s]
        out_ref[s, sz.grad_rows :, :] = ends_ref[s]


def unpack_kernel(sz, in_ref, ends_out, gx_out, gy_out, gz_out, norm_out, rows):
    lane = lane_of((SUB, LANES))

    def whole_tile(tile, row, slot):
        result = None
        for q in range(sz.factor):
            block = tile * sz.factor + q
            part = roll_lanes(in_ref[block, row : row + SUB, :], sz.own * (q - slot))
            result = part if result is None else jnp.where(lane < sz.own * q, result, part)
        return result

    for t in range(sz.nz // LANES):
        columns = slice(t * LANES, (t + 1) * LANES)
        for p in range(sz.planes):
            for n in range(sz.grad_parts):
                f, r = divmod(n, sz.share)
                row = (p * sz.grad_tiles + n // sz.factor) * SUB
                (gx_out, gy_out, gz_out)[f][p, r * SUB : (r + 1) * SUB, columns] = whole_tile(t, row, n % sz.factor)
            for n in range(sz.end_parts):
                row = sz.grad_rows + (p * sz.end_tiles + n // sz.factor) * SUB
                rows[t, p, pl.ds(n, SUB, stride=sz.tiles), :] = whole_tile(t, row, n % sz.factor)
            ends_out[0, p, :, columns] = rows[t, p]
    squares = in_ref[0, sz.grad_rows + sz.end_rows :, :]
    for s in range(1, sz.space):
        squares = squares + in_ref[s, sz.grad_rows + sz.end_rows :, :]
    cells = (sz.spans - 1) * sz.nx * (sz.ny // 2) * (sz.nz // 2)
    whole = jnp.sum(jnp.sum(squares, axis=1, keepdims=True), axis=0, keepdims=True)
    norm_out[...] = jnp.sqrt(whole / cells)


def f32(*shape):
    return jax.ShapeDtypeStruct(shape, jnp.float32)


def call(kernel, sz, outs, scratch, *args, name, cost=None):
    held = sum(4 * math.prod(shape) for shape in scratch)
    held += sum(4 * math.prod(array.shape) for array in jax.tree.leaves((outs, args)))
    return pl.pallas_call(
        functools.partial(kernel, sz),
        out_shape=outs,
        scratch_shapes=[pltpu.VMEM(shape, jnp.float32) for shape in scratch],
        compiler_params=pltpu.CompilerParams(vmem_limit_bytes=held + SPARE_BYTES),
        cost_estimate=cost,
        name=name,
    )(*args)


def windows(kernel, sz, out, columns, *args, name):
    return pl.pallas_call(
        functools.partial(kernel, sz),
        out_shape=out,
        in_specs=[pl.BlockSpec(memory_space=pltpu.HBM)] * len(args),
        scratch_shapes=[pltpu.VMEM(array.shape, array.dtype) for array in args]
        + [pltpu.VMEM(columns, jnp.float32), pltpu.SemaphoreType.DMA((len(args),))],
        compiler_params=pltpu.CompilerParams(vmem_limit_bytes=60 * 1024 * 1024),
        name=name,
    )(*args)


def turned(index, size):
    result = 0
    while size > 1:
        result, index, size = result * 2 + index % 2, index // 2, size // 2
    return result


def exchange(values, axis, bit):
    size = lax.axis_size(axis)
    return lax.ppermute(values, axis, [(i, i ^ bit) for i in range(size)])


def from_all(values, axis):
    pieces, bit = {0: values}, lax.axis_size(axis) // 2
    while bit:
        for key, piece in list(pieces.items()):
            pieces[key | bit] = exchange(piece, axis, bit)
        bit //= 2
    return [pieces[key] for key in range(len(pieces))]


def shards(start_states, diff_x, diff_y, diff_z, stress, trap_class, cotangent):
    spans, space = lax.axis_size("tm"), lax.axis_size("space")
    sz = Sizes(spans, space, *diff_x.shape)
    nx, ny = sz.nx, sz.ny
    columns = (sz.planes, sz.nz // LANES, ny, LANES)
    coef = windows(
        face_windows_kernel,
        sz,
        f32(space, 4 * sz.planes * sz.quarter, LANES),
        (4,) + columns,
        diff_x,
        diff_y,
        diff_z,
        stress,
        trap_class,
        name="face_windows",
    )
    both = windows(
        field_windows_kernel,
        sz,
        f32(space, (sz.start_tiles + sz.cot_tiles) * SUB, LANES),
        (2,) + columns,
        start_states,
        cotangent,
        name="field_windows",
    )
    coef = lax.all_to_all(coef, "space", 0, 0)
    both = lax.all_to_all(both, "space", 0, 0)

    pieces = from_all(coef, "tm")

    tiles = sz.tiles
    rough_shape = f32(nx, tiles // 4, SUB, LANES)
    rough = call(rough_kernel, sz, rough_shape, (), both, name="rough")
    following = lax.ppermute(rough, "tm", [(i + 1, i) for i in range(spans - 1)])

    def field(count, *front):
        return front + (count, SUB, LANES)

    coefs, scales = call(
        factors_kernel,
        sz,
        (f32(*field(tiles, 6, nx)), f32(*field(tiles, 2, nx))),
        (field(tiles, 4, nx),),
        *pieces,
        name="factors",
        cost=pl.CostEstimate(flops=40 * nx * ny * LANES, bytes_accessed=12 * 4 * nx * ny * LANES, transcendentals=0),
    )
    end, jumps, grads = call(
        fine_kernel,
        sz,
        (f32(*field(tiles, nx)), rough_shape, f32(spans, space, sz.grad_rows, LANES)),
        (
            field(tiles, 3, nx),
            field(tiles + 2, nx),
            field(tiles + 2, nx),
            field(tiles + 2, nx),
            field(tiles + 2, nx),
            field(tiles + 1, TOTAL + 1, nx + 1),
            field(tiles + 1, TOTAL, nx + 1),
        ),
        coefs,
        scales,
        both,
        following,
        name="fine",
    )
    jumps = from_all(jumps, "tm")

    half, bit = spans // 2, 1
    while half:
        come = exchange(grads[half:], "tm", bit)
        kept = grads[:half]
        grads = kept + come if half > 1 else None
        half, bit = half // 2, bit * 2

    half_tiles = tiles // 2
    coarse_coefs, coarse_scales = call(
        coarse_factors_kernel,
        sz,
        (f32(*field(half_tiles, 6, nx)), f32(*field(half_tiles, 2, nx))),
        (field(tiles, 4, nx), field(half_tiles, 4, nx)),
        *pieces,
        name="coarse_factors",
    )
    ends = call(
        coarse_kernel,
        sz,
        f32(space, sz.end_rows + SUB, LANES),
        (
            field(half_tiles + 2, nx),
            field(half_tiles + 2, nx),
            field(half_tiles, nx),
            field(tiles // 4, spans, nx),
        ),
        coarse_coefs,
        coarse_scales,
        *jumps,
        end,
        name="coarse",
    )
    joined = call(join_kernel, sz, f32(space, sz.out_rows, LANES), (), kept, come, ends, name="join")
    joined = lax.all_to_all(joined, "space", 0, 0)
    quarter = f32(sz.planes, sz.quarter, sz.nz)
    new_end, gx, gy, gz, norm = call(
        unpack_kernel,
        sz,
        (f32(1, sz.planes, ny, sz.nz), quarter, quarter, quarter, f32(1, 1)),
        ((sz.nz // LANES, sz.planes, ny, LANES),),
        joined,
        name="unpack",
    )
    return new_end, gx, gy, gz, norm.reshape(())


def solution(mesh):
    fields = P("tm", "space", None, None)
    faces = P("space", None, None)
    quarter = P("space", "tm", None)
    return jax.shard_map(
        shards,
        mesh=mesh,
        in_specs=(fields, faces, faces, faces, faces, faces, fields),
        out_specs=(fields, quarter, quarter, quarter, P()),
        check_vma=False,
    )
```
